32 devices in a mesh: groups: 2 (over x), cells: 4 (over y, core), blocks: 4 (over z).
Axes of the slice: x: 2, y: 2, z: 4, core: 2. Of those that a mesh axis runs over, the one named last changes fastest.
Arguments:
- expression: bfloat16 [8192, 4096], P(('groups', 'cells'), 'blocks'), parts along dimension 0, as said below
Outputs:
- adjacency: float32 [8192, 4096], P(('groups', 'blocks'), 'cells'), parts along dimension 0
There are 2 independent parts, one for each index of `groups`. The reference program is written for one: setup_inputs(seed, part) draws one part's arguments, and reference() takes and returns one part's arrays. A program takes and returns all parts, laid end to end along the dimension named above; each array names one. Nothing has to cross between parts.
Inputs may be any that keep to these rules, and one draw needn't show every extreme that they name: `expression`: every gene has a nonzero noise part, so every variance is positive.
All inputs are finite; a program needn't handle non-finite values.
Results may differ from the reference program's by a relative error of at most 0.0003.
Values sent between devices are 32-bit elements; how exact they have to be, the bound alone decides.
No kernel may reach another device: no remote copies, remote signals or barrier semaphores. Data moves between devices by JAX's collectives and lax.ppermute only.
A program may use at most 128 MiB of HBM per device.

```python
import math
import jax
import jax.numpy as jnp
from jax import lax

GENES = 4096
MODULES = 16
CELLS = 4096


def draw_expression(key, part):
    key = jax.random.fold_in(key, 11)
    keys = jax.random.split(key, 8)
    module = jax.random.randint(keys[0], (GENES,), 0, MODULES)
    loading = jax.random.uniform(keys[1], (GENES,), jnp.float32, -1.5, 1.5)
    noise_scale = jnp.exp(jax.random.uniform(keys[2], (GENES,), jnp.float32, math.log(0.3), math.log(1.5)))
    position = jnp.arange(CELLS, dtype=jnp.float32) / (CELLS - 1)
    ramp = 1.0 + 2.0 * position
    depth = ramp * jnp.exp(0.3 * jax.random.normal(keys[3], (CELLS,), jnp.float32))
    factors = jax.random.normal(keys[4], (CELLS, MODULES), jnp.float32)
    trend = 1.5 * jax.random.normal(keys[7], (GENES,), jnp.float32)
    offset = 3.0 * jax.random.normal(keys[5], (GENES,), jnp.float32)
    noise = jax.random.normal(keys[6], (CELLS, GENES), jnp.float32)
    rising = 1.0 + 3.0 * position
    signal = jnp.take(factors, module, axis=1) * loading[None, :]
    level = offset[None, :] + rising[:, None] * trend[None, :]
    return (depth[:, None] * (signal + noise_scale[None, :] * noise) + level).astype(jnp.bfloat16)


def setup_inputs(seed: int = 0, part: int = 0) -> dict:
    splits = jax.random.split(jax.random.key(seed), 2)
    part_splits = jax.random.split(jax.random.fold_in(splits[1], part), 2)
    return {
        "expression": draw_expression(jax.random.fold_in(jax.random.fold_in(splits[1], part), 71), part),
    }


def reference(expression):
    values = expression.astype(jnp.float32)
    mean = lax.optimization_barrier(jnp.sum(values, axis=0)) / CELLS
    centred = values - mean[None, :]
    gram = jnp.dot(centred.T, centred, preferred_element_type=jnp.float32, precision=lax.Precision.HIGHEST)
    variance = lax.optimization_barrier(jnp.sum(centred * centred, axis=0))
    ratio = gram / jnp.sqrt(variance[:, None] * variance[None, :])
    return ((1.0 + ratio) / 2.0) ** 6
```

```python
import functools

import jax
import jax.numpy as jnp
from jax import lax
from jax.experimental import pallas as pl
from jax.experimental.pallas import tpu as pltpu
from jax.sharding import PartitionSpec as P

BOTH = ("cells", "blocks")
TILE = 256
FAR_WIDTHS = (2, 1, 1)
f32, bf16 = jnp.float32, jnp.bfloat16
ANYWHERE = pl.BlockSpec(memory_space=pl.ANY)


def call(kernel, *, grid, in_specs, out_specs, out_shape, scratch=(), scalars=0, aliases=None):
    return pl.pallas_call(
        kernel,
        grid_spec=pltpu.PrefetchScalarGridSpec(
            num_scalar_prefetch=scalars,
            grid=grid,
            in_specs=in_specs,
            out_specs=out_specs,
            scratch_shapes=scratch,
        ),
        out_shape=out_shape,
        input_output_aliases=aliases or {},
        cost_estimate=pl.CostEstimate(flops=1, bytes_accessed=1, transcendentals=0),
        compiler_params=pltpu.CompilerParams(vmem_limit_bytes=48 << 20),
    )


def shape(*dims):
    return jax.ShapeDtypeStruct(dims, f32)


def split(value):
    high = value.astype(bf16)
    return high, (value - high.astype(f32)).astype(bf16)


def centre_kernel(x_ref, centred_ref, turned_ref, mean_ref, spread_ref):
    value = x_ref[...].astype(f32)
    mean = jnp.sum(value, axis=0, keepdims=True) / value.shape[0]
    value = value - mean
    centred_ref[...] = value
    turned_ref[...] = value.T
    mean_ref[...] = mean
    spread_ref[...] = jnp.sum(value * value, axis=0, keepdims=True)


def centre(expression):
    rows, width = expression.shape
    column = pl.BlockSpec((rows, TILE), lambda g: (0, g))
    line = pl.BlockSpec((1, TILE), lambda g: (0, g))
    return call(
        centre_kernel,
        grid=(width // TILE,),
        in_specs=[column],
        out_specs=[column, pl.BlockSpec((TILE, rows), lambda g: (g, 0)), line, line],
        out_shape=[shape(rows, width), shape(width, rows), shape(1, width), shape(1, width)],
    )(expression)


def copy_kernel(from_ref, *refs):
    refs[-1][...] = from_ref[...]


def columns(source, start, size, *earlier):
    rows = source.shape[0]
    return call(
        copy_kernel,
        grid=(rows // TILE,),
        in_specs=[pl.BlockSpec((TILE, size), lambda i: (i, start // size))]
        + [ANYWHERE] * len(earlier),
        out_specs=pl.BlockSpec((TILE, size), lambda i: (i, 0)),
        out_shape=shape(rows, size),
    )(source, *earlier)


def three(left, right, contract):
    def dot(a, b):
        return lax.dot_general(a, b, (contract, ((), ())), preferred_element_type=f32)

    (left_high, left_low), (right_high, right_low) = left, right
    return dot(left_high, right_high) + (dot(left_high, right_low) + dot(left_low, right_high))


def spans(width):
    return [slice(start, min(start + 512, width)) for start in range(0, width, 512)]


def own_kernel(turned_ref, out_ref, high_ref, low_ref):
    step = pl.program_id(0)

    @pl.when(step == 0)
    def _():
        high_ref[...], low_ref[...] = split(turned_ref[...])

    rows = pl.ds(pl.multiple_of(step * TILE, TILE), TILE)
    left = high_ref[rows], low_ref[rows]
    for span in spans(out_ref.shape[1]):
        out_ref[:, span] = three(left, (high_ref[span], low_ref[span]), ((1,), (1,)))


def own_gram(turned):
    width, cells = turned.shape
    whole = pl.BlockSpec((width, cells), lambda i: (0, 0))
    out_sum, *parts = call(
        own_kernel,
        grid=(width // TILE,),
        in_specs=[whole],
        out_specs=[pl.BlockSpec((TILE, width), lambda i: (i, 0)), whole, whole],
        out_shape=[shape(width, width)] + [jax.ShapeDtypeStruct((width, cells), bf16)] * 2,
    )(turned)
    return out_sum, parts


def pair_kernel(left_high, left_low, right_high, right_low, *refs):
    out_ref = refs[-1]
    left = left_high[...], left_low[...]
    for span in spans(out_ref.shape[1]):
        out_ref[:, span] = three(left, (right_high[span], right_low[span]), ((1,), (1,)))


def pair_gram(own, pair, *earlier):
    width, cells = own[0].shape
    whole = pl.BlockSpec((width, cells), lambda i: (0, 0))
    return call(
        pair_kernel,
        grid=(width // TILE,),
        in_specs=[pl.BlockSpec((TILE, cells), lambda i: (i, 0))] * 2
        + [whole] * 2
        + [ANYWHERE] * len(earlier),
        out_specs=pl.BlockSpec((TILE, width), lambda i: (i, 0)),
        out_shape=shape(width, width),
    )(*own, *pair, *earlier)


def both_kernel(pair_is_split, core_ref, own_high, own_low, *refs):
    right_high, right_low = refs[-2:]
    if pair_is_split:
        pair_high, pair_low, right_ref = refs[:3]
        out_ref = refs[-3]
        pair = pair_high[...], pair_low[...]
    else:
        pair_ref, right_ref = refs[:2]
        out_ref, pair_high, pair_low = refs[-5:-2]
        pair = split(pair_ref[...])
        pair_high[...], pair_low[...] = pair

    @pl.when(pl.program_id(0) == 0)
    def _():
        right_high[...], right_low[...] = split(right_ref[...])

    core = core_ref[0]
    for span in spans(out_ref.shape[2]):
        right = right_high[:, span], right_low[:, span]
        out_ref[core, :, span] = three((own_high[...], own_low[...]), right, ((1,), (0,)))
        out_ref[1 - core, :, span] = three(pair, right, ((1,), (0,)))


def both_grams(core, own, pair, right, *earlier):
    width, cells = own[0].shape
    size = right.shape[1]
    left = pl.BlockSpec((TILE, cells), lambda i, core: (i, 0))
    is_split = len(pair) == 2
    extra = 0 if is_split else 2
    out = call(
        functools.partial(both_kernel, is_split),
        scalars=1,
        grid=(width // TILE,),
        in_specs=[left] * (2 + len(pair))
        + [pl.BlockSpec((cells, size), lambda i, core: (0, 0))]
        + [ANYWHERE] * len(earlier),
        out_specs=[pl.BlockSpec((2, TILE, size), lambda i, core: (0, i, 0))] + [left] * extra,
        out_shape=[shape(2, width, size)]
        + [jax.ShapeDtypeStruct((width, cells), bf16)] * extra,
        scratch=[pltpu.VMEM((cells, size), bf16)] * 2,
    )(core, *own, *pair, right, *earlier)
    return out[0], (pair if is_split else out[1:])


def power_six(ratio):
    half = (1.0 + ratio) * 0.5
    square = half * half
    return square * square * square


def finish_kernel(flags, *refs):
    own, own_far, pair, pair_far, mid, mid_first, mid_second, far, far_first, far_second = refs[:10]
    rs, cs, offset = refs[10:13]
    out_ref = refs[-1]
    for kind, (left, other, right) in enumerate(
        ((own, own, own_far), (pair, pair, pair_far), (mid, mid_second, mid_first), (far, far_second, far_first))
    ):
        for outer in range(2) if kind > 1 else (None,):
            now = flags[0] == kind
            if outer is not None:
                now &= flags[1] == outer

            @pl.when(now)
            def _():
                tile = (other if outer else left)[...] + right[...]
                out_ref[...] = power_six(tile * rs[...] * cs[...] + offset[...])


def finish(flags, near, mid, far, scales, before, start, mid_start):
    (row_scale, column_scale, offset), (width, size) = scales, far[0].shape

    def spec(column, kinds, outer=None):
        def index(i, flags):
            used = flags[0] == kinds
            if outer is not None:
                used &= flags[1] == outer
            return jnp.where(used, i, 0), column

        return pl.BlockSpec((TILE, size), index)

    column, mid_column = start // size, (start - mid_start) // size
    here = pl.BlockSpec((TILE, size), lambda i, flags: (i, column))
    in_specs = [spec(column, 0)] * 2 + [spec(column, 1)] * 2
    in_specs += [spec(mid_column, 2, 0), spec(mid_column, 2), spec(mid_column, 2, 1)]
    in_specs += [spec(0, 3, 0), spec(0, 3), spec(0, 3, 1)]
    in_specs += [
        pl.BlockSpec((TILE, 1), lambda i, flags: (i, 0)),
        pl.BlockSpec((1, size), lambda i, flags: (0, column)),
        here,
    ]
    operands = [flags, *near, *mid, *far, row_scale, column_scale, offset]
    aliases = {}
    if before is not None:
        aliases = {len(operands): 0}
        in_specs.append(ANYWHERE)
        operands.append(before)
    return call(
        finish_kernel,
        scalars=1,
        grid=(width // TILE,),
        in_specs=in_specs,
        out_specs=here,
        out_shape=shape(*offset.shape),
        aliases=aliases,
    )(*operands)


def cross_gram(left, right):
    return lax.dot_general(
        left,
        right,
        (((0,), (0,)), ((), ())),
        preferred_element_type=f32,
        precision=lax.Precision.HIGH,
    )


def pieces(width, shares):
    unit = width // sum(shares)
    starts = [unit * sum(shares[:i]) for i in range(len(shares))]
    return [(start, unit * share) for start, share in zip(starts, shares)]


def local_statistics(values):
    mean = jnp.sum(values, axis=0) / values.shape[0]
    shifted = values - mean[None, :]
    return shifted, mean, jnp.sum(shifted * shifted, axis=0)


def statistics(rows, mean, spread):
    shards = lax.all_gather(jnp.stack([mean, spread]), "cells")
    away = shards[:, 0] - jnp.mean(shards[:, 0], axis=0)[None, :]
    variance = jnp.sum(shards[:, 1], axis=0) + rows * jnp.sum(away * away, axis=0)
    return away, variance


def on_a_line(expression):
    rows, width = expression.shape
    z = lax.axis_index("blocks")
    k = lax.axis_index("cells")
    mid_of, far_of = (2, 2, 1, 1), (3, 3, 0, 0)
    own_owner, pair_owner = (0, 1, 2, 3), (1, 0, 3, 2)
    mid_id, far_id = jnp.where(z < 2, 2, 1), jnp.where(z < 2, 3, 0)
    outer = (z == 0) | (z == 3)
    kind = jnp.where(k == z, 0, jnp.where(k == (z ^ 1), 1, jnp.where(k == mid_id, 2, 3)))
    flags = jnp.stack([kind, outer.astype(kind.dtype)]).astype(jnp.int32)
    mid_core, far_core = (mid_id % 2).astype(jnp.int32)[None], (far_id % 2).astype(jnp.int32)[None]

    def between(part, pairs, name):
        with jax.named_scope(name):
            return lax.ppermute(part, BOTH, [(a * 4 + b, c * 4 + d) for (a, b), (c, d) in pairs])

    def along(part, pairs, name):
        with jax.named_scope(name):
            return lax.ppermute(part, "blocks", pairs)

    def to_core(part, owner, name):
        pairs = [(2 * y + owner[b] % 2, b) for y in range(2) for b in range(4)]
        return part + between(part, [((i ^ 1, b), (i, b)) for i, b in pairs], name)

    def to_lane(part, owner, name):
        return between(part, [((owner[b] ^ 2, b), (owner[b], b)) for b in range(4)], name)

    def over_cores(parts):
        got = lax.all_to_all(parts, "cells", 0, 0, axis_index_groups=[[0, 1], [2, 3]], tiled=True)
        return got[0] + got[1]

    def onward(part, owner, name):
        first = [((owner[b] ^ 2, b), (owner[b], b)) for b in (1, 2)]
        first += [((owner[b] ^ 3, b), (owner[b], b ^ 1)) for b in (1, 2)]
        second = [((owner[b] ^ 1, b), (owner[b], b ^ 1)) for b in (1, 2)]
        return between(part, first, name + "_first"), between(part, second, name + "_second")

    centred, turned, mean, spread = centre(expression)
    mid_got = along(centred, [(1, 2), (2, 1)], "mid_block")
    pair_got = along(turned, [(0, 1), (1, 0), (2, 3), (3, 2)], "pair_block")
    far = pieces(width, FAR_WIDTHS)

    def send_far(part, *earlier):
        value = columns(centred, *far[part], *earlier)
        return along(value, [(0, 2), (3, 1)], "far_block")

    own_sum, own = own_gram(turned)
    far_got = [send_far(0, own_sum)]
    own_sum = to_core(own_sum, own_owner, "own_core")
    own_far = to_lane(own_sum, own_owner, "own_lane")
    away, variance = statistics(rows, mean[0], spread[0])
    mine = jnp.concatenate([away, variance[None, :], jnp.zeros((3, width), f32)])
    column = jnp.where(k == z, mine, 0.0)
    for by in (1, 2, 3):
        column += between(mine, [((i, i), (i, (i + by) % 4)) for i in range(4)], "moments")
    far_got.append(send_far(1, column))

    parts, pair = both_grams(mid_core, own, (pair_got,), mid_got, own_far, column)
    mid_sum = over_cores(parts)
    mid = (mid_sum, *onward(mid_sum, mid_of, "mid_sum"))
    pair_sum = pair_gram(own, pair, parts)
    last = (mid_sum, pair_sum)
    far_got.append(send_far(2, pair_sum))
    pair_sum = to_core(pair_sum, pair_owner, "pair_core")
    pair_far = to_lane(pair_sum, pair_owner, "pair_lane")
    fars = []
    waits = [(), mid[1:], (pair_far,)]
    for got, wait in zip(far_got, waits):
        parts, _ = both_grams(far_core, own, pair, got, *last, *wait)
        far_sum = over_cores(parts)
        last = (far_sum,)
        fars.append((far_sum, *onward(far_sum, far_of, "far_sum")))

    row_scale = 1.0 / jnp.sqrt(variance)
    column_scale = 1.0 / jnp.sqrt(column[4])
    offset = rows * lax.dot_general(
        away * row_scale[None, :],
        column[:4] * column_scale[None, :],
        (((0,), (0,)), ((), ())),
        precision=lax.Precision.HIGHEST,
    )
    scales = (row_scale[:, None], column_scale[None, :], offset)
    result = None
    for tile, (start, size) in zip(fars, far):
        near = (own_sum, own_far, pair_sum, pair_far)
        result = finish(flags, near, mid, tile, scales, result, start, 0)
    return result


def on_a_ring(expression):
    rows, width = expression.shape
    block_count = lax.axis_size("blocks")
    shifted, mean, spread = local_statistics(expression.astype(jnp.float32))
    away, variance = statistics(rows, mean, spread)
    centred = shifted + lax.dynamic_index_in_dim(away, lax.axis_index("cells"), 0)
    every_variance = lax.all_gather(variance, "blocks", axis=0, tiled=True)
    mine = lax.axis_index("blocks")
    partial_value = jnp.zeros((width, width * block_count), jnp.float32)
    current = centred
    for step in range(block_count):
        if step > 0:
            ring = [(i, (i + 1) % block_count) for i in range(block_count)]
            current = lax.ppermute(current, "blocks", ring)
        source = (mine - step) % block_count
        partial_value = lax.dynamic_update_slice_in_dim(
            partial_value, cross_gram(centred, current), source * width, 1
        )
    tile = lax.psum_scatter(partial_value, "cells", scatter_dimension=1, tiled=True)
    column_start = lax.axis_index("cells") * tile.shape[1]
    column_variance = lax.dynamic_slice_in_dim(every_variance, column_start, tile.shape[1])
    row_scale, column_scale = 1.0 / jnp.sqrt(variance), 1.0 / jnp.sqrt(column_variance)
    return power_six(tile * row_scale[:, None] * column_scale[None, :])


def solution(mesh):
    line = mesh.shape["cells"] == 4 and mesh.shape["blocks"] == 4
    return jax.shard_map(
        on_a_line if line else on_a_ring,
        mesh=mesh,
        in_specs=(P(("groups", "cells"), "blocks"),),
        out_specs=P(("groups", "blocks"), "cells"),
        check_vma=False,
    )
```

```python
import functools

import jax
import jax.numpy as jnp
from jax import lax
from jax.experimental import pallas as pl
from jax.experimental.pallas import tpu as pltpu
from jax.sharding import PartitionSpec as P

BOTH = ("cells", "blocks")
TILE = 256
FAR_WIDTHS = (1, 1)
PAD = 16
f32, bf16 = jnp.float32, jnp.bfloat16
ANYWHERE = pl.BlockSpec(memory_space=pl.ANY)


def call(kernel, *, grid, in_specs, out_specs, out_shape, scratch=(), scalars=0, aliases=None, flops=1):
    return pl.pallas_call(
        kernel,
        grid_spec=pltpu.PrefetchScalarGridSpec(
            num_scalar_prefetch=scalars,
            grid=grid,
            in_specs=in_specs,
            out_specs=out_specs,
            scratch_shapes=scratch,
        ),
        out_shape=out_shape,
        input_output_aliases=aliases or {},
        cost_estimate=pl.CostEstimate(flops=flops, bytes_accessed=1, transcendentals=0),
        compiler_params=pltpu.CompilerParams(vmem_limit_bytes=48 << 20),
    )


def shape(*dims):
    return jax.ShapeDtypeStruct(dims, f32)


def split(value):
    high = value.astype(bf16)
    return high, (value - high.astype(f32)).astype(bf16)


def centre_kernel(x_ref, centred_ref, turned_ref, mean_ref, spread_ref):
    value = x_ref[...].astype(f32)
    mean = jnp.sum(value, axis=0, keepdims=True) / value.shape[0]
    value = value - mean
    centred_ref[...] = value
    turned_ref[...] = value.T
    mean_ref[...] = mean
    spread_ref[...] = jnp.sum(value * value, axis=0, keepdims=True)


def centre(expression):
    rows, width = expression.shape
    column = pl.BlockSpec((rows, TILE), lambda g: (0, g))
    line = pl.BlockSpec((1, TILE), lambda g: (0, g))
    return call(
        centre_kernel,
        grid=(width // TILE,),
        in_specs=[column],
        out_specs=[column, pl.BlockSpec((TILE, rows), lambda g: (g, 0)), line, line],
        out_shape=[shape(rows, width), shape(width, rows), shape(1, width), shape(1, width)],
    )(expression)


def copy_kernel(from_ref, *refs):
    refs[-1][...] = from_ref[...]


def columns(source, start, size, *earlier):
    rows = source.shape[0]
    tile = (rows + PAD) // 2
    return call(
        copy_kernel,
        grid=(2,),
        in_specs=[pl.BlockSpec((tile, size), lambda i: (i, start // size))]
        + [ANYWHERE] * len(earlier),
        out_specs=pl.BlockSpec((tile, size), lambda i: (i, 0)),
        out_shape=shape(rows + PAD, size),
    )(source, *earlier)


def gram_kernel(roles, turned, role_ref, *refs):
    lefts, rights = refs[: 2 * roles], refs[2 * roles : 2 * roles + 2]
    out_ref, left_high, left_low, right_high, right_low = refs[-5:]
    cells = lefts[0].shape[1]

    @pl.when(pl.program_id(0) == 0)
    def _():
        for core, ref in enumerate(rights):
            span = slice(core * cells, (core + 1) * cells)
            at = (slice(None), span) if turned else span
            right_high[at], right_low[at] = split(ref[...])

    for role in range(roles):

        @pl.when(role_ref[0] == role if roles > 1 else True)
        def _():
            for core in range(2):
                at = (slice(None), slice(core * cells, (core + 1) * cells))
                left_high[at], left_low[at] = split(lefts[2 * role + core][...])

    contract = (((1,), (1 if turned else 0,)), ((), ()))

    def dot(left, right):
        return lax.dot_general(left, right, contract, preferred_element_type=f32)

    width = out_ref.shape[1]
    for start in range(0, width, 512):
        span = slice(start, min(start + 512, width))
        at = span if turned else (slice(None), span)
        high, low = right_high[at], right_low[at]
        out_ref[:, span] = dot(left_high[...], high) + (
            dot(left_high[...], low) + dot(left_low[...], high)
        )


def gram(role, lefts, rights, turned, earlier, columns=None):
    width, cells = lefts[0].shape
    roles = len(lefts) // 2
    start, size = (0, width) if turned else columns or (0, rights[0].shape[1])

    def left_spec(of_role):
        def index(i, role_ref):
            return (jnp.where(role_ref[0] == of_role, i, 0) if roles > 1 else i), 0

        return pl.BlockSpec((TILE, cells), index)

    right_block = (width, cells) if turned else (cells, size)
    right_shape = (width, 2 * cells) if turned else (2 * cells, size)
    return call(
        functools.partial(gram_kernel, roles, turned),
        scalars=1,
        grid=(width // TILE,),
        in_specs=[left_spec(n // 2) for n in range(len(lefts))]
        + [pl.BlockSpec(right_block, lambda i, role_ref: (0, start // size))] * 2
        + [ANYWHERE] * len(earlier),
        out_specs=pl.BlockSpec((TILE, size), lambda i, role_ref: (i, 0)),
        out_shape=shape(width, size),
        scratch=[pltpu.VMEM((TILE, 2 * cells), bf16)] * 2 + [pltpu.VMEM(right_shape, bf16)] * 2,
    )(role, *lefts, *rights, *earlier)


def together(work, *given):
    like = jax.eval_shape(work, *given)
    zeros = lambda *_: jax.tree.map(lambda leaf: jnp.zeros(leaf.shape, leaf.dtype), like)
    return lax.cond(lax.axis_index("cells") >= 0, work, zeros, *given)


def power_six(ratio):
    half = (1.0 + ratio) * 0.5
    square = half * half
    return square * square * square


def add_kernel(*refs):
    refs[-1][...] = refs[0][...] + refs[1][...]


def add(left, right, *earlier):
    block = pl.BlockSpec((TILE, left.shape[1]), lambda i: (i, 0))
    return call(
        add_kernel,
        grid=(left.shape[0] // TILE,),
        in_specs=[block] * 2 + [ANYWHERE] * len(earlier),
        out_specs=block,
        out_shape=shape(*left.shape),
    )(left, right, *earlier)


def base_kernel(kinds, flags, *refs):
    sums, (rs, cs, offset), out_ref = refs[: len(kinds)], refs[len(kinds) : len(kinds) + 3], refs[-1]
    for kind in sorted(set(kind for used, _ in kinds for kind in used)):

        @pl.when(flags[0] == kind)
        def _():
            tiles = {}
            for ref, (used, start) in zip(sums, kinds):
                if kind in used:
                    tiles.setdefault(start, []).append(ref)
            for start, (left, *rights) in tiles.items():
                at = (slice(None), slice(start, start + left.shape[1]))
                right = rights[0][...]
                if len(rights) > 1:
                    right = jnp.where(2 * pl.program_id(0) < pl.num_programs(0), right, rights[1][...])
                ratio = (left[...] + right) * rs[...] * cs[at] + offset[at]
                out_ref[at] = power_six(ratio)


def base(flags, sums, scales, *earlier):
    width = scales[2].shape[0]
    arrays, kinds = [array for array, _, _ in sums], [(used, start) for _, used, start in sums]

    def spec(array, used):
        steps = array.shape[0] // TILE

        def index(i, flags):
            mine = functools.reduce(jnp.logical_or, [flags[0] == kind for kind in used])
            return jnp.where(mine, i % steps, 0), 0

        return pl.BlockSpec((TILE, array.shape[1]), index)

    here = pl.BlockSpec((TILE, width), lambda i, flags: (i, 0))
    return call(
        functools.partial(base_kernel, kinds),
        scalars=1,
        grid=(width // TILE,),
        in_specs=[spec(array, used) for array, used, _ in sums]
        + [
            pl.BlockSpec((TILE, 1), lambda i, flags: (i, 0)),
            pl.BlockSpec((1, width), lambda i, flags: (0, 0)),
            here,
        ]
        + [ANYWHERE] * len(earlier),
        out_specs=here,
        out_shape=shape(width, width),
    )(flags, *arrays, *scales, *earlier)


def finish_kernel(flags, merged, first, second, rs, cs, offset, before, out_ref):
    @pl.when(flags[1] == 0)
    def _():
        out_ref[...] = before[...]

    for outer, left in enumerate((merged, second)):

        @pl.when(flags[1] == 1 + outer)
        def _():
            tile = left[...] + first[...]
            out_ref[...] = power_six(tile * rs[...] * cs[...] + offset[...])


def finish(flags, far, scales, before, start):
    (row_scale, column_scale, offset), (width, size) = scales, far[0].shape
    column = start // size
    whole = pl.BlockSpec((TILE, size), lambda i, flags: (i, 0))
    here = pl.BlockSpec((TILE, size), lambda i, flags: (i, column))
    operands = [flags, *far, row_scale, column_scale, offset, before]
    return call(
        finish_kernel,
        scalars=1,
        grid=(width // TILE,),
        in_specs=[whole] * 3
        + [
            pl.BlockSpec((TILE, 1), lambda i, flags: (i, 0)),
            pl.BlockSpec((1, size), lambda i, flags: (0, column)),
            here,
            here,
        ],
        out_specs=here,
        out_shape=shape(width, width),
        aliases={len(operands) - 1: 0},
    )(*operands)


def cross_gram(left, right):
    return lax.dot_general(
        left,
        right,
        (((0,), (0,)), ((), ())),
        preferred_element_type=f32,
        precision=lax.Precision.HIGH,
    )


def pieces(width, shares):
    unit = width // sum(shares)
    starts = [unit * sum(shares[:i]) for i in range(len(shares))]
    return [(start, unit * share) for start, share in zip(starts, shares)]


def local_statistics(values):
    mean = jnp.sum(values, axis=0) / values.shape[0]
    shifted = values - mean[None, :]
    return shifted, mean, jnp.sum(shifted * shifted, axis=0)


def statistics(rows, mean, spread):
    shards = lax.all_gather(jnp.stack([mean, spread]), "cells")
    away = shards[:, 0] - jnp.mean(shards[:, 0], axis=0)[None, :]
    variance = jnp.sum(shards[:, 1], axis=0) + rows * jnp.sum(away * away, axis=0)
    return away, variance


def on_a_line(expression):
    rows, width = expression.shape
    z = lax.axis_index("blocks")
    k = lax.axis_index("cells")
    mid_of, far_of = (2, 2, 1, 1), (3, 3, 0, 0)
    own_owner, pair_owner = (0, 1, 2, 3), (1, 0, 3, 2)
    far_id = jnp.where(z < 2, 3, 0)
    outer = ((z == 0) | (z == 3)).astype(jnp.int32)
    kind = jnp.where(k == far_id, 4, 2) + outer
    kind = jnp.where(k == z, 0, jnp.where(k == (z ^ 1), 1, kind))
    flags = jnp.stack([kind, jnp.where(k == far_id, 1 + outer, 0)]).astype(jnp.int32)
    far_role = (k % 2 != far_id % 2).astype(jnp.int32)[None]
    mid_role = 1 - far_role

    def between(part, pairs, name):
        with jax.named_scope(name):
            return lax.ppermute(part, BOTH, [(a * 4 + b, c * 4 + d) for (a, b), (c, d) in pairs])

    def along(part, pairs, name):
        with jax.named_scope(name):
            return lax.ppermute(part, "blocks", pairs)

    def other(part, name):
        return between(part, [((i, b), (i ^ 1, b)) for i in range(4) for b in range(4)], name)

    def to_lane(part, owner, name):
        return between(part, [((owner[b] ^ 2, b), (owner[b], b)) for b in range(4)], name)

    def in_halves(part, owner, name):
        half = width // 2
        return [to_lane(part[:half], owner, name), to_lane(part[half:], owner, name)]

    def onward(part, owner, name):
        pairs = [((owner[b] ^ 2, b), (owner[b], b)) for b in (1, 2)]
        pairs += [((owner[b] ^ 3, b), (owner[b], b ^ 1)) for b in (1, 2)]
        pairs += [((owner[b] ^ 1, b), (owner[b] ^ 1, b ^ 1)) for b in (1, 2)]
        return between(part, pairs, name)

    def folded(part, owner, name):
        return between(part, [((owner[b] ^ 1, b), (owner[b], b)) for b in (0, 3)], name)

    centred, turned, mean, spread = centre(expression)
    mid_got = along(centred, [(1, 2), (2, 1)], "mid_block")
    pair_got = along(turned, [(0, 1), (1, 0), (2, 3), (3, 2)], "pair_block")
    far = pieces(width, FAR_WIDTHS)
    away, variance = statistics(rows, mean[0], spread[0])
    mine = jnp.concatenate([away, variance[None, :], jnp.zeros((11, width), f32)])

    def own_work(turned, mine):
        own = turned, other(turned, "own_other")
        return gram(mid_role, own, own, True, (mine,)), own[1]

    def mid_work(own, pair_got, mid_got, earlier):
        pair = pair_got, other(pair_got, "pair_other")
        right = mid_got, other(mid_got, "mid_other")
        return gram(mid_role, own + pair, right, False, earlier), pair[1]

    def far_work(own, pair, got, earlier):
        right = got, other(got, "far_other")
        return gram(far_role, own + pair, right, False, earlier)

    own_sum, own_other = together(own_work, turned, mine)
    own = turned, own_other
    pairs = [((a, b), (b, a)) for a in range(4) for b in range(4) if a != b]
    column = between(mine, pairs, "moments")
    far_got = []
    for start, size in far:
        part = columns(centred, start, size, pair_got, mid_got, column)
        far_got.append(along(part, [(0, 2), (3, 1)], "far_block"))
    own_far = to_lane(own_sum, own_owner, "own_lane")
    mid_sum, pair_other = together(mid_work, own, pair_got, mid_got, (own_sum,))
    pair = pair_got, pair_other
    mid_far = onward(mid_sum, mid_of, "mid_sum")
    pair_sum = gram(mid_role, own, pair, True, (mid_sum,))
    pair_far = in_halves(pair_sum, pair_owner, "pair_lane")
    waits = [(own_far,), ()]
    far_sums, last = [], pair_sum
    for part, wait in enumerate(waits):
        last = together(far_work, own, pair, far_got[part], (last, *wait))
        sent = jnp.pad(last, ((0, PAD), (0, 0))) if part == 0 else last
        far_sums.append((last, onward(sent, far_of, "far_sum")))

    column = jnp.where(k == z, mine, column)
    row_scale = 1.0 / jnp.sqrt(variance)
    column_scale = 1.0 / jnp.sqrt(column[4])
    offset = rows * lax.dot_general(
        away * row_scale[None, :],
        column[:4] * column_scale[None, :],
        (((0,), (0,)), ((), ())),
        precision=lax.Precision.HIGHEST,
    )
    scales = (row_scale[:, None], column_scale[None, :], offset)

    def base_work(near, mid, fars, scales):
        sums = [(array, (n // 2 if n < 4 else 1,), 0) for n, array in enumerate(near)]
        sums += [(mid[0], (2,), 0), (mid[1], (2, 3), 0), (folded(mid[1], mid_of, "mid_fold"), (3,), 0)]
        for (total, got), (start, _) in zip(fars, far):
            fold = folded(got, far_of, "far_fold")
            sums += [(total, (4,), start), (got, (4, 5), start), (fold, (5,), start)]
        return base(flags, sums, scales)

    def last_base_work(tile, scales, result):
        tile = (*tile, folded(tile[1], far_of, "far_fold"))
        return finish(flags, tile, scales, result, far[-1][0])

    near = own_sum, own_far, pair_sum, *pair_far
    result = together(base_work, near, (mid_sum, mid_far), far_sums[:-1], scales)
    return together(last_base_work, far_sums[-1], scales, result)


def on_a_ring(expression):
    rows, width = expression.shape
    block_count = lax.axis_size("blocks")
    shifted, mean, spread = local_statistics(expression.astype(jnp.float32))
    away, variance = statistics(rows, mean, spread)
    centred = shifted + lax.dynamic_index_in_dim(away, lax.axis_index("cells"), 0)
    every_variance = lax.all_gather(variance, "blocks", axis=0, tiled=True)
    mine = lax.axis_index("blocks")
    partial_value = jnp.zeros((width, width * block_count), jnp.float32)
    current = centred
    for step in range(block_count):
        if step > 0:
            ring = [(i, (i + 1) % block_count) for i in range(block_count)]
            current = lax.ppermute(current, "blocks", ring)
        source = (mine - step) % block_count
        partial_value = lax.dynamic_update_slice_in_dim(
            partial_value, cross_gram(centred, current), source * width, 1
        )
    tile = lax.psum_scatter(partial_value, "cells", scatter_dimension=1, tiled=True)
    column_start = lax.axis_index("cells") * tile.shape[1]
    column_variance = lax.dynamic_slice_in_dim(every_variance, column_start, tile.shape[1])
    row_scale, column_scale = 1.0 / jnp.sqrt(variance), 1.0 / jnp.sqrt(column_variance)
    return power_six(tile * row_scale[:, None] * column_scale[None, :])


def solution(mesh):
    line = mesh.shape["cells"] == 4 and mesh.shape["blocks"] == 4
    return jax.shard_map(
        on_a_line if line else on_a_ring,
        mesh=mesh,
        in_specs=(P(("groups", "cells"), "blocks"),),
        out_specs=P(("groups", "blocks"), "cells"),
        check_vma=False,
    )
```

```python
import functools

import jax
import jax.numpy as jnp
from jax import lax
from jax.experimental import pallas as pl
from jax.experimental.pallas import tpu as pltpu
from jax.sharding import PartitionSpec as P

BOTH = ("cells", "blocks")
TILE = 256
FAR_WIDTHS = (1, 1)
PAD = 16
f32, bf16 = jnp.float32, jnp.bfloat16
ANYWHERE = pl.BlockSpec(memory_space=pl.ANY)


def call(kernel, *, grid, in_specs, out_specs, out_shape, scratch=(), scalars=0, aliases=None, flops=1):
    return pl.pallas_call(
        kernel,
        grid_spec=pltpu.PrefetchScalarGridSpec(
            num_scalar_prefetch=scalars,
            grid=grid,
            in_specs=in_specs,
            out_specs=out_specs,
            scratch_shapes=scratch,
        ),
        out_shape=out_shape,
        input_output_aliases=aliases or {},
        cost_estimate=pl.CostEstimate(flops=flops, bytes_accessed=1, transcendentals=0),
        compiler_params=pltpu.CompilerParams(vmem_limit_bytes=48 << 20),
    )


def shape(*dims):
    return jax.ShapeDtypeStruct(dims, f32)


def split(value):
    high = value.astype(bf16)
    return high, (value - high.astype(f32)).astype(bf16)


def centre_kernel(x_ref, centred_ref, turned_ref, mean_ref, spread_ref):
    value = x_ref[...].astype(f32)
    mean = jnp.sum(value, axis=0, keepdims=True) / value.shape[0]
    value = value - mean
    centred_ref[...] = value
    turned_ref[...] = value.T
    mean_ref[...] = mean
    spread_ref[...] = jnp.sum(value * value, axis=0, keepdims=True)


def centre(expression):
    rows, width = expression.shape
    column = pl.BlockSpec((rows, TILE), lambda g: (0, g))
    line = pl.BlockSpec((1, TILE), lambda g: (0, g))
    return call(
        centre_kernel,
        grid=(width // TILE,),
        in_specs=[column],
        out_specs=[column, pl.BlockSpec((TILE, rows), lambda g: (g, 0)), line, line],
        out_shape=[shape(rows, width), shape(width, rows), shape(1, width), shape(1, width)],
    )(expression)


def copy_kernel(from_ref, *refs):
    refs[-1][...] = from_ref[...]


def columns(source, start, size, *earlier):
    rows = source.shape[0]
    tile = (rows + PAD) // 2
    return call(
        copy_kernel,
        grid=(2,),
        in_specs=[pl.BlockSpec((tile, size), lambda i: (i, start // size))]
        + [ANYWHERE] * len(earlier),
        out_specs=pl.BlockSpec((tile, size), lambda i: (i, 0)),
        out_shape=shape(rows + PAD, size),
    )(source, *earlier)


def gram_kernel(roles, turned, role_ref, *refs):
    lefts, rights = refs[: 2 * roles], refs[2 * roles : 2 * roles + 2]
    out_ref, left_high, left_low, right_high, right_low = refs[-5:]
    cells = lefts[0].shape[1]

    @pl.when(pl.program_id(0) == 0)
    def _():
        for core, ref in enumerate(rights):
            span = slice(core * cells, (core + 1) * cells)
            at = (slice(None), span) if turned else span
            right_high[at], right_low[at] = split(ref[...])

    for role in range(roles):

        @pl.when(role_ref[0] == role if roles > 1 else True)
        def _():
            for core in range(2):
                at = (slice(None), slice(core * cells, (core + 1) * cells))
                left_high[at], left_low[at] = split(lefts[2 * role + core][...])

    contract = (((1,), (1 if turned else 0,)), ((), ()))

    def dot(left, right):
        return lax.dot_general(left, right, contract, preferred_element_type=f32)

    width = out_ref.shape[1]
    for start in range(0, width, 512):
        span = slice(start, min(start + 512, width))
        at = span if turned else (slice(None), span)
        high, low = right_high[at], right_low[at]
        out_ref[:, span] = dot(left_high[...], high) + (
            dot(left_high[...], low) + dot(left_low[...], high)
        )


def gram(role, lefts, rights, turned, earlier, rows=None, pad=0):
    width, cells = lefts[0].shape
    roles, rows = len(lefts) // 2, rows or width
    size = rights[0].shape[0 if turned else 1]

    def left_spec(of_role):
        def index(i, role_ref):
            at = i + role_ref[1]
            return (jnp.where(role_ref[0] == of_role, at, 0) if roles > 1 else at), 0

        return pl.BlockSpec((TILE, cells), index)

    right_block = (size, cells) if turned else (cells, size)
    right_shape = (size, 2 * cells) if turned else (2 * cells, size)
    return call(
        functools.partial(gram_kernel, roles, turned),
        scalars=1,
        grid=(rows // TILE,),
        in_specs=[left_spec(n // 2) for n in range(len(lefts))]
        + [pl.BlockSpec(right_block, lambda i, role_ref: (0, 0))] * 2
        + [ANYWHERE] * len(earlier),
        out_specs=pl.BlockSpec((TILE, size), lambda i, role_ref: (i, 0)),
        out_shape=shape(rows + pad, size),
        scratch=[pltpu.VMEM((TILE, 2 * cells), bf16)] * 2 + [pltpu.VMEM(right_shape, bf16)] * 2,
    )(role, *lefts, *rights, *earlier)


def together(work, *given):
    like = jax.eval_shape(work, *given)
    zeros = lambda *_: jax.tree.map(lambda leaf: jnp.zeros(leaf.shape, leaf.dtype), like)
    return lax.cond(lax.axis_index("cells") >= 0, work, zeros, *given)


def power_six(ratio):
    half = (1.0 + ratio) * 0.5
    square = half * half
    return square * square * square


def add_kernel(*refs):
    refs[-1][...] = refs[0][...] + refs[1][...]


def add(left, right, *earlier):
    block = pl.BlockSpec((TILE, left.shape[1]), lambda i: (i, 0))
    return call(
        add_kernel,
        grid=(left.shape[0] // TILE,),
        in_specs=[block] * 2 + [ANYWHERE] * len(earlier),
        out_specs=block,
        out_shape=shape(*left.shape),
    )(left, right, *earlier)


def base_kernel(kinds, flags, *refs):
    sums, (rs, cs, offset), out_ref = refs[: len(kinds)], refs[len(kinds) : len(kinds) + 3], refs[-1]
    for kind in sorted(set(kind for used, _ in kinds for kind in used)):

        @pl.when(flags[0] == kind)
        def _():
            tiles = {}
            for ref, (used, start) in zip(sums, kinds):
                if kind in used:
                    tiles.setdefault(start, []).append(ref)
            for start, (left, right) in tiles.items():
                at = (slice(None), slice(start, start + left.shape[1]))
                tile = left[...] + right[...]
                if kind == 1:
                    half = 2 * pl.program_id(0) // pl.num_programs(0)
                    tile = jnp.where(flags[2] == half, left[...], right[...])
                out_ref[at] = power_six(tile * rs[...] * cs[at] + offset[at])


def base(flags, sums, scales, *earlier):
    width = scales[2].shape[0]
    arrays, kinds = [array for array, _, _ in sums], [(used, start) for _, used, start in sums]

    def spec(array, used):
        steps = array.shape[0] // TILE

        def index(i, flags):
            mine = functools.reduce(jnp.logical_or, [flags[0] == kind for kind in used])
            return jnp.where(mine, i % steps, 0), 0

        return pl.BlockSpec((TILE, array.shape[1]), index)

    here = pl.BlockSpec((TILE, width), lambda i, flags: (i, 0))
    return call(
        functools.partial(base_kernel, kinds),
        scalars=1,
        grid=(width // TILE,),
        in_specs=[spec(array, used) for array, used, _ in sums]
        + [
            pl.BlockSpec((TILE, 1), lambda i, flags: (i, 0)),
            pl.BlockSpec((1, width), lambda i, flags: (0, 0)),
            here,
        ]
        + [ANYWHERE] * len(earlier),
        out_specs=here,
        out_shape=shape(width, width),
    )(flags, *arrays, *scales, *earlier)


def finish_kernel(flags, merged, first, second, rs, cs, offset, before, out_ref):
    @pl.when(flags[1] == 0)
    def _():
        out_ref[...] = before[...]

    for outer, left in enumerate((merged, second)):

        @pl.when(flags[1] == 1 + outer)
        def _():
            tile = left[...] + first[...]
            out_ref[...] = power_six(tile * rs[...] * cs[...] + offset[...])


def finish(flags, far, scales, before, start):
    (row_scale, column_scale, offset), (width, size) = scales, far[0].shape
    column = start // size
    whole = pl.BlockSpec((TILE, size), lambda i, flags: (i, 0))
    here = pl.BlockSpec((TILE, size), lambda i, flags: (i, column))
    operands = [flags, *far, row_scale, column_scale, offset, before]
    return call(
        finish_kernel,
        scalars=1,
        grid=(width // TILE,),
        in_specs=[whole] * 3
        + [
            pl.BlockSpec((TILE, 1), lambda i, flags: (i, 0)),
            pl.BlockSpec((1, size), lambda i, flags: (0, column)),
            here,
            here,
        ],
        out_specs=here,
        out_shape=shape(width, width),
        aliases={len(operands) - 1: 0},
    )(*operands)


def cross_gram(left, right):
    return lax.dot_general(
        left,
        right,
        (((0,), (0,)), ((), ())),
        preferred_element_type=f32,
        precision=lax.Precision.HIGH,
    )


def pieces(width, shares):
    unit = width // sum(shares)
    starts = [unit * sum(shares[:i]) for i in range(len(shares))]
    return [(start, unit * share) for start, share in zip(starts, shares)]


def local_statistics(values):
    mean = jnp.sum(values, axis=0) / values.shape[0]
    shifted = values - mean[None, :]
    return shifted, mean, jnp.sum(shifted * shifted, axis=0)


def statistics(rows, mean, spread):
    shards = lax.all_gather(jnp.stack([mean, spread]), "cells")
    away = shards[:, 0] - jnp.mean(shards[:, 0], axis=0)[None, :]
    variance = jnp.sum(shards[:, 1], axis=0) + rows * jnp.sum(away * away, axis=0)
    return away, variance


def on_a_line(expression):
    rows, width = expression.shape
    z = lax.axis_index("blocks")
    k = lax.axis_index("cells")
    mid_of, far_of = (2, 2, 1, 1), (3, 3, 0, 0)
    own_owner, pair_owner = (0, 1, 2, 3), (1, 0, 3, 2)
    far_id = jnp.where(z < 2, 3, 0)
    outer = ((z == 0) | (z == 3)).astype(jnp.int32)
    kind = jnp.where(k == far_id, 4, 2) + outer
    kind = jnp.where(k == z, 0, jnp.where(k == (z ^ 1), 1, kind))
    flags = jnp.stack([kind, jnp.where(k == far_id, 1 + outer, 0), k % 2]).astype(jnp.int32)
    far_role = jnp.stack([(k % 2 != far_id % 2).astype(jnp.int32), 0])
    mid_role = jnp.stack([1 - far_role[0], 0])
    pair_half = jnp.stack([0, (k % 2) * (width // 2 // TILE)]).astype(jnp.int32)

    def between(part, pairs, name):
        with jax.named_scope(name):
            return lax.ppermute(part, BOTH, [(a * 4 + b, c * 4 + d) for (a, b), (c, d) in pairs])

    def along(part, pairs, name):
        with jax.named_scope(name):
            return lax.ppermute(part, "blocks", pairs)

    def other(part, name):
        return between(part, [((i, b), (i ^ 1, b)) for i in range(4) for b in range(4)], name)

    def to_lane(part, owner, name, cores=(0,)):
        pairs = [((owner[b] ^ 2 ^ c, b), (owner[b] ^ c, b)) for b in range(4) for c in cores]
        return between(part, pairs, name)

    def onward(part, owner, name):
        pairs = [((owner[b] ^ 2, b), (owner[b], b)) for b in (1, 2)]
        pairs += [((owner[b] ^ 3, b), (owner[b], b ^ 1)) for b in (1, 2)]
        pairs += [((owner[b] ^ 1, b), (owner[b] ^ 1, b ^ 1)) for b in (1, 2)]
        return between(part, pairs, name)

    def folded(part, owner, name):
        return between(part, [((owner[b] ^ 1, b), (owner[b], b)) for b in (0, 3)], name)

    centred, turned, mean, spread = centre(expression)
    mid_got = along(centred, [(1, 2), (2, 1)], "mid_block")
    pair_got = along(turned, [(0, 1), (1, 0), (2, 3), (3, 2)], "pair_block")
    far = pieces(width, FAR_WIDTHS)
    away, variance = statistics(rows, mean[0], spread[0])
    mine = jnp.concatenate([away, variance[None, :], jnp.zeros((11, width), f32)])

    def own_work(turned, mine):
        own = turned, other(turned, "own_other")
        return gram(mid_role, own, own, True, (mine,)), own[1]

    def mid_work(own, pair_got, mid_got, earlier):
        pair = pair_got, other(pair_got, "pair_other")
        right = mid_got, other(mid_got, "mid_other")
        return gram(mid_role, own + pair, right, False, earlier), pair[1]

    def far_work(own, pair, got, earlier, pad):
        right = got, other(got, "far_other")
        return gram(far_role, own + pair, right, False, earlier, pad=pad)

    own_sum, own_other = together(own_work, turned, mine)
    own = turned, own_other
    pairs = [((a, b), (b, a)) for a in range(4) for b in range(4) if a != b]
    column = between(mine, pairs, "moments")
    far_got = []
    for start, size in far:
        part = columns(centred, start, size, pair_got, mid_got, column)
        far_got.append(along(part, [(0, 2), (3, 1)], "far_block"))
    own_far = to_lane(own_sum, own_owner, "own_lane")
    mid_sum, pair_other = together(mid_work, own, pair_got, mid_got, (own_sum,))
    pair = pair_got, pair_other
    mid_far = onward(mid_sum, mid_of, "mid_sum")
    pair_sum = gram(pair_half, own, pair, True, (mid_sum,), rows=width // 2, pad=PAD)
    pair_far = to_lane(pair_sum, pair_owner, "pair_lane", cores=(0, 1))
    waits = [(own_far,), ()]
    far_sums, last = [], pair_sum
    for part, wait in enumerate(waits):
        work = functools.partial(far_work, pad=PAD if part == 0 else 0)
        last = together(work, own, pair, far_got[part], (last, *wait))
        far_sums.append((last, onward(last, far_of, "far_sum")))

    column = jnp.where(k == z, mine, column)
    row_scale = 1.0 / jnp.sqrt(variance)
    column_scale = 1.0 / jnp.sqrt(column[4])
    offset = rows * lax.dot_general(
        away * row_scale[None, :],
        column[:4] * column_scale[None, :],
        (((0,), (0,)), ((), ())),
        precision=lax.Precision.HIGHEST,
    )
    scales = (row_scale[:, None], column_scale[None, :], offset)

    def base_work(near, mid, fars, scales):
        own_sum, own_far, pair_sum, pair_far = near
        pair_sum += pair_far
        sums = [(own_sum, (0,), 0), (own_far, (0,), 0)]
        sums += [(pair_sum, (1,), 0), (other(pair_sum, "pair_fold"), (1,), 0)]
        sums += [(mid[0], (2,), 0), (mid[1], (2, 3), 0), (folded(mid[1], mid_of, "mid_fold"), (3,), 0)]
        for (total, got), (start, _) in zip(fars, far):
            fold = folded(got, far_of, "far_fold")
            sums += [(total, (4,), start), (got, (4, 5), start), (fold, (5,), start)]
        return base(flags, sums, scales)

    def last_base_work(tile, scales, result):
        tile = (*tile, folded(tile[1], far_of, "far_fold"))
        return finish(flags, tile, scales, result, far[-1][0])

    near = own_sum, own_far, pair_sum, pair_far
    result = together(base_work, near, (mid_sum, mid_far), far_sums[:-1], scales)
    return together(last_base_work, far_sums[-1], scales, result)


def on_a_ring(expression):
    rows, width = expression.shape
    block_count = lax.axis_size("blocks")
    shifted, mean, spread = local_statistics(expression.astype(jnp.float32))
    away, variance = statistics(rows, mean, spread)
    centred = shifted + lax.dynamic_index_in_dim(away, lax.axis_index("cells"), 0)
    every_variance = lax.all_gather(variance, "blocks", axis=0, tiled=True)
    mine = lax.axis_index("blocks")
    partial_value = jnp.zeros((width, width * block_count), jnp.float32)
    current = centred
    for step in range(block_count):
        if step > 0:
            ring = [(i, (i + 1) % block_count) for i in range(block_count)]
            current = lax.ppermute(current, "blocks", ring)
        source = (mine - step) % block_count
        partial_value = lax.dynamic_update_slice_in_dim(
            partial_value, cross_gram(centred, current), source * width, 1
        )
    tile = lax.psum_scatter(partial_value, "cells", scatter_dimension=1, tiled=True)
    column_start = lax.axis_index("cells") * tile.shape[1]
    column_variance = lax.dynamic_slice_in_dim(every_variance, column_start, tile.shape[1])
    row_scale, column_scale = 1.0 / jnp.sqrt(variance), 1.0 / jnp.sqrt(column_variance)
    return power_six(tile * row_scale[:, None] * column_scale[None, :])


def solution(mesh):
    line = mesh.shape["cells"] == 4 and mesh.shape["blocks"] == 4
    return jax.shard_map(
        on_a_line if line else on_a_ring,
        mesh=mesh,
        in_specs=(P(("groups", "cells"), "blocks"),),
        out_specs=P(("groups", "blocks"), "cells"),
        check_vma=False,
    )
```

```python
import functools

import jax
import jax.numpy as jnp
from jax import lax
from jax.experimental import pallas as pl
from jax.experimental.pallas import tpu as pltpu
from jax.sharding import PartitionSpec as P

BOTH = ("cells", "blocks")
TILE = 256
FAR_WIDTHS = (1, 1)
PAD = 16
f32, bf16 = jnp.float32, jnp.bfloat16
ANYWHERE = pl.BlockSpec(memory_space=pl.ANY)


def call(kernel, *, grid, in_specs, out_specs, out_shape, scratch=(), scalars=0, aliases=None, flops=1):
    return pl.pallas_call(
        kernel,
        grid_spec=pltpu.PrefetchScalarGridSpec(
            num_scalar_prefetch=scalars,
            grid=grid,
            in_specs=in_specs,
            out_specs=out_specs,
            scratch_shapes=scratch,
        ),
        out_shape=out_shape,
        input_output_aliases=aliases or {},
        cost_estimate=pl.CostEstimate(flops=flops, bytes_accessed=1, transcendentals=0),
        compiler_params=pltpu.CompilerParams(vmem_limit_bytes=48 << 20),
    )


def shape(*dims):
    return jax.ShapeDtypeStruct(dims, f32)


def split(value):
    high = value.astype(bf16)
    return high, (value - high.astype(f32)).astype(bf16)


def centre_kernel(x_ref, centred_ref, turned_ref, mean_ref, spread_ref):
    value = x_ref[...].astype(f32)
    mean = jnp.sum(value, axis=0, keepdims=True) / value.shape[0]
    value = value - mean
    centred_ref[...] = value
    turned_ref[...] = value.T
    mean_ref[...] = mean
    spread_ref[...] = jnp.sum(value * value, axis=0, keepdims=True)


def centre(expression):
    rows, width = expression.shape
    column = pl.BlockSpec((rows, TILE), lambda g: (0, g))
    line = pl.BlockSpec((1, TILE), lambda g: (0, g))
    return call(
        centre_kernel,
        grid=(width // TILE,),
        in_specs=[column],
        out_specs=[column, pl.BlockSpec((TILE, rows), lambda g: (g, 0)), line, line],
        out_shape=[shape(rows, width), shape(width, rows), shape(1, width), shape(1, width)],
    )(expression)


def copy_kernel(from_ref, to_ref):
    to_ref[...] = from_ref[...]


def columns(source, start, size):
    rows = source.shape[0]
    tile = (rows + PAD) // 2
    return call(
        copy_kernel,
        grid=(2,),
        in_specs=[pl.BlockSpec((tile, size), lambda i: (i, start // size))],
        out_specs=pl.BlockSpec((tile, size), lambda i: (i, 0)),
        out_shape=shape(rows + PAD, size),
    )(source)


def pass_on(value, *earlier):
    return call(
        lambda *refs: None,
        grid=(1,),
        in_specs=[ANYWHERE] * (1 + len(earlier)),
        out_specs=ANYWHERE,
        out_shape=shape(*value.shape),
        aliases={0: 0},
    )(value, *earlier)


def gram_kernel(roles, turned, role_ref, *refs):
    lefts, rights = refs[: 2 * roles], refs[2 * roles : 2 * roles + 2]
    out_ref, left_high, left_low, right_high, right_low = refs[-5:]
    cells = lefts[0].shape[1]

    @pl.when(pl.program_id(0) == 0)
    def _():
        for core, ref in enumerate(rights):
            span = slice(core * cells, (core + 1) * cells)
            at = (slice(None), span) if turned else span
            right_high[at], right_low[at] = split(ref[...])

    for role in range(roles):

        @pl.when(role_ref[0] == role if roles > 1 else True)
        def _():
            for core in range(2):
                at = (slice(None), slice(core * cells, (core + 1) * cells))
                left_high[at], left_low[at] = split(lefts[2 * role + core][...])

    contract = (((1,), (1 if turned else 0,)), ((), ()))

    def dot(left, right):
        return lax.dot_general(left, right, contract, preferred_element_type=f32)

    width = out_ref.shape[1]
    for start in range(0, width, 512):
        span = slice(start, min(start + 512, width))
        at = span if turned else (slice(None), span)
        high, low = right_high[at], right_low[at]
        out_ref[:, span] = dot(left_high[...], high) + (
            dot(left_high[...], low) + dot(left_low[...], high)
        )


def gram(role, lefts, rights, turned, earlier, rows=None, pad=0):
    width, cells = lefts[0].shape
    roles, rows = len(lefts) // 2, rows or width
    size = rights[0].shape[0 if turned else 1]

    def left_spec(of_role):
        def index(i, role_ref):
            at = i + role_ref[1]
            return (jnp.where(role_ref[0] == of_role, at, 0) if roles > 1 else at), 0

        return pl.BlockSpec((TILE, cells), index)

    right_block = (size, cells) if turned else (cells, size)
    right_shape = (size, 2 * cells) if turned else (2 * cells, size)
    return call(
        functools.partial(gram_kernel, roles, turned),
        scalars=1,
        grid=(rows // TILE,),
        in_specs=[left_spec(n // 2) for n in range(len(lefts))]
        + [pl.BlockSpec(right_block, lambda i, role_ref: (0, 0))] * 2
        + [ANYWHERE] * len(earlier),
        out_specs=pl.BlockSpec((TILE, size), lambda i, role_ref: (i, 0)),
        out_shape=shape(rows + pad, size),
        scratch=[pltpu.VMEM((TILE, 2 * cells), bf16)] * 2 + [pltpu.VMEM(right_shape, bf16)] * 2,
    )(role, *lefts, *rights, *earlier)


def together(work, *given):
    like = jax.eval_shape(work, *given)
    zeros = lambda *_: jax.tree.map(lambda leaf: jnp.zeros(leaf.shape, leaf.dtype), like)
    return lax.cond(lax.axis_index("cells") >= 0, work, zeros, *given)


def power_six(ratio):
    half = (1.0 + ratio) * 0.5
    square = half * half
    return square * square * square


def add_kernel(*refs):
    refs[-1][...] = refs[0][...] + refs[1][...]


def add(left, right, *earlier):
    block = pl.BlockSpec((TILE, left.shape[1]), lambda i: (i, 0))
    return call(
        add_kernel,
        grid=(left.shape[0] // TILE,),
        in_specs=[block] * 2 + [ANYWHERE] * len(earlier),
        out_specs=block,
        out_shape=shape(*left.shape),
    )(left, right, *earlier)


def adjacency(left, right, rs, cs, row_moments, column_moments):
    between_shards = sum(row_moments[:, n : n + 1] * column_moments[n : n + 1] for n in range(4))
    return power_six((left + right) * rs * cs + between_shards)


def scale_specs(size, column):
    return [
        pl.BlockSpec((TILE, 1), lambda i, flags: (i, 0)),
        pl.BlockSpec((1, size), lambda i, flags: (0, column)),
        pl.BlockSpec((TILE, 8), lambda i, flags: (i, 0)),
        pl.BlockSpec((8, size), lambda i, flags: (0, column)),
    ]


def base_kernel(pieces, flags, *refs):
    (rs, cs, rm, cm, out_ref), refs = refs[-5:], iter(refs)
    in_first = 2 * pl.program_id(0) < pl.num_programs(0)
    for start, halves in pieces:
        left, right = next(refs)[...], next(refs)[...]
        if halves:
            left = jnp.where(in_first, left, next(refs)[...])
            right = jnp.where(in_first, right, next(refs)[...])
        at = (slice(None), slice(start, start + left.shape[1]))
        out_ref[at] = adjacency(left, right, rs[...], cs[at], rm[...], cm[at])


def base(flags, pieces, scales):
    width = scales[0].shape[0]
    arrays = [array for _, *parts in pieces for array in parts]

    def spec(array):
        steps = array.shape[0] // TILE
        return pl.BlockSpec((TILE, array.shape[1]), lambda i, flags: (i % steps, 0))

    return call(
        functools.partial(base_kernel, [(start, len(parts) == 4) for start, *parts in pieces]),
        scalars=1,
        grid=(width // TILE,),
        in_specs=[spec(array) for array in arrays] + scale_specs(width, 0),
        out_specs=pl.BlockSpec((TILE, width), lambda i, flags: (i, 0)),
        out_shape=shape(width, width),
    )(flags, *arrays, *scales)


def finish_kernel(flags, merged, first, second, rs, cs, rm, cm, before, out_ref):
    @pl.when(flags[1] == 0)
    def _():
        out_ref[...] = before[...]

    for outer, left in enumerate((merged, second)):

        @pl.when(flags[1] == 1 + outer)
        def _():
            out_ref[...] = adjacency(left[...], first[...], rs[...], cs[...], rm[...], cm[...])


def finish(flags, far, scales, before, start):
    width, size = before.shape[0], far[0].shape[1]
    here = pl.BlockSpec((TILE, size), lambda i, flags: (i, start // size))

    def spec(*kinds, column=0):
        def index(i, flags):
            used = functools.reduce(jnp.logical_or, [flags[1] == kind for kind in kinds])
            return jnp.where(used, i, 0), column

        return pl.BlockSpec((TILE, size), index)

    operands = [flags, *far, *scales, before]
    return call(
        finish_kernel,
        scalars=1,
        grid=(width // TILE,),
        in_specs=[spec(1), spec(1, 2), spec(2)]
        + scale_specs(size, start // size)
        + [spec(0, column=start // size)],
        out_specs=here,
        out_shape=shape(width, width),
        aliases={len(operands) - 1: 0},
    )(*operands)


def cross_gram(left, right):
    return lax.dot_general(
        left,
        right,
        (((0,), (0,)), ((), ())),
        preferred_element_type=f32,
        precision=lax.Precision.HIGH,
    )


def pieces(width, shares):
    unit = width // sum(shares)
    starts = [unit * sum(shares[:i]) for i in range(len(shares))]
    return [(start, unit * share) for start, share in zip(starts, shares)]


def local_statistics(values):
    mean = jnp.sum(values, axis=0) / values.shape[0]
    shifted = values - mean[None, :]
    return shifted, mean, jnp.sum(shifted * shifted, axis=0)


def statistics(rows, mean, spread):
    shards = lax.all_gather(jnp.stack([mean, spread]), "cells")
    away = shards[:, 0] - jnp.mean(shards[:, 0], axis=0)[None, :]
    variance = jnp.sum(shards[:, 1], axis=0) + rows * jnp.sum(away * away, axis=0)
    return away, variance


def on_a_line(expression):
    rows, width = expression.shape
    z = lax.axis_index("blocks")
    k = lax.axis_index("cells")
    mid_of, far_of = (2, 2, 1, 1), (3, 3, 0, 0)
    own_owner, pair_owner = (0, 1, 2, 3), (1, 0, 3, 2)
    far_id = jnp.where(z < 2, 3, 0)
    outer = ((z == 0) | (z == 3)).astype(jnp.int32)
    kind = jnp.where(k == far_id, 5, 3) + outer
    kind = jnp.where(k == z, 0, jnp.where(k == (z ^ 1), 1 + k % 2, kind))
    flags = jnp.stack([kind, jnp.where(k == far_id, 1 + outer, 0)]).astype(jnp.int32)
    far_role = jnp.stack([(k % 2 != far_id % 2).astype(jnp.int32), 0])
    mid_role = jnp.stack([1 - far_role[0], 0])
    pair_half = jnp.stack([0, (k % 2) * (width // 2 // TILE)]).astype(jnp.int32)

    def between(part, pairs, name):
        with jax.named_scope(name):
            return lax.ppermute(part, BOTH, [(a * 4 + b, c * 4 + d) for (a, b), (c, d) in pairs])

    def along(part, pairs, name):
        with jax.named_scope(name):
            return lax.ppermute(part, "blocks", pairs)

    def other(part, name):
        return between(part, [((i, b), (i ^ 1, b)) for i in range(4) for b in range(4)], name)

    def to_lane(part, owner, name, cores=(0,)):
        pairs = [((owner[b] ^ 2 ^ c, b), (owner[b] ^ c, b)) for b in range(4) for c in cores]
        return between(part, pairs, name)

    def onward(part, owner, name):
        pairs = [((owner[b] ^ 2, b), (owner[b], b)) for b in (1, 2)]
        pairs += [((owner[b] ^ 3, b), (owner[b], b ^ 1)) for b in (1, 2)]
        pairs += [((owner[b] ^ 1, b), (owner[b] ^ 1, b ^ 1)) for b in (1, 2)]
        return between(part, pairs, name)

    def directly(part, owner, name):
        first = [((owner[b] ^ 2, b), (owner[b], b)) for b in (1, 2)]
        first += [((owner[b] ^ 3, b), (owner[b], b ^ 1)) for b in (1, 2)]
        second = [((owner[b] ^ 1, b), (owner[b], b ^ 1)) for b in (1, 2)]
        return between(part, first, name + "_first"), between(part, second, name + "_second")

    def folded(part, owner, name):
        return between(part, [((owner[b] ^ 1, b), (owner[b], b)) for b in (0, 3)], name)

    centred, turned, mean, spread = centre(expression)
    mid_got = along(centred, [(1, 2), (2, 1)], "mid_block")
    pair_got = along(turned, [(0, 1), (1, 0), (2, 3), (3, 2)], "pair_block")
    far = pieces(width, FAR_WIDTHS)
    far_parts = [columns(centred, *piece) for piece in far]
    away, variance = statistics(rows, mean[0], spread[0])
    mine = jnp.concatenate([away, variance[None, :], jnp.zeros((11, width), f32)])

    def own_work(turned, earlier):
        own = turned, other(turned, "own_other")
        return gram(mid_role, own, own, True, earlier), own[1]

    def mid_work(own, pair_got, mid_got, earlier):
        pair = pair_got, other(pair_got, "pair_other")
        right = mid_got, other(mid_got, "mid_other")
        return gram(mid_role, own + pair, right, False, earlier), pair[1]

    def first_far_work(own, pair, got, pair_sum, earlier):
        right = got, other(got, "far_other")
        total = gram(far_role, own + pair, right, False, earlier, pad=PAD)
        return total, other(pass_on(pair_sum, right[1]), "pair_fold")

    def last_far_work(own, pair, got, earlier):
        right = got, other(got, "far_other")
        return gram(far_role, own + pair, right, False, earlier)

    own_sum, own_other = together(own_work, turned, (mine, *far_parts))
    own = turned, own_other
    pairs = [((a, b), (b, a)) for a in range(4) for b in range(4) if a != b]
    column = between(mine, pairs, "moments")
    far_got = []
    for part in far_parts:
        part = pass_on(part, pair_got, mid_got, column)
        far_got.append(along(part, [(0, 2), (3, 1)], "far_block"))
    own_far = to_lane(own_sum, own_owner, "own_lane")
    mid_sum, pair_other = together(mid_work, own, pair_got, mid_got, (own_sum,))
    pair = pair_got, pair_other
    mid_far = onward(mid_sum, mid_of, "mid_sum")
    pair_sum = gram(pair_half, own, pair, True, (mid_sum,), rows=width // 2, pad=PAD)
    pair_far = to_lane(pair_sum, pair_owner, "pair_lane", cores=(0, 1))
    first_sum, pair_fold = together(
        first_far_work, own, pair, far_got[0], pair_sum, (pair_sum, own_far)
    )
    first_far = onward(first_sum, far_of, "far_sum")
    last_sum = together(last_far_work, own, pair, far_got[1], (first_sum,))
    last_far = directly(last_sum, far_of, "far_sum")

    column = jnp.where(k == z, mine, column)
    row_scale = 1.0 / jnp.sqrt(variance)
    column_scale = 1.0 / jnp.sqrt(column[4])
    row_moments = rows * jnp.pad(away * row_scale[None, :], ((0, 4), (0, 0))).T
    column_moments = jnp.pad(column[:4] * column_scale[None, :], ((0, 4), (0, 0)))
    scales = row_scale[:, None], column_scale[None, :], row_moments, column_moments

    def base_work(near, mid, far, scales):
        own_sum, own_far, pair_sum, pair_far, pair_fold = near
        pair_far_fold = other(pair_far, "pair_fold")
        cases = [
            [(0, own_sum, own_far)],
            [(0, pair_sum, pair_far, pair_fold, pair_far_fold)],
            [(0, pair_fold, pair_far_fold, pair_sum, pair_far)],
            [(0, *mid)],
            [(0, folded(mid[1], mid_of, "mid_fold"), mid[1])],
            [(0, *far)],
            [(0, folded(far[1], far_of, "far_fold"), far[1])],
        ]
        return lax.switch(flags[0], [lambda case=case: base(flags, case, scales) for case in cases])

    near = own_sum, own_far, pair_sum, pair_far, pair_fold
    result = together(base_work, near, (mid_sum, mid_far), (first_sum, first_far), scales)
    return finish(flags, (last_sum, *last_far), scales, result, far[1][0])


def on_a_ring(expression):
    rows, width = expression.shape
    block_count = lax.axis_size("blocks")
    shifted, mean, spread = local_statistics(expression.astype(jnp.float32))
    away, variance = statistics(rows, mean, spread)
    centred = shifted + lax.dynamic_index_in_dim(away, lax.axis_index("cells"), 0)
    every_variance = lax.all_gather(variance, "blocks", axis=0, tiled=True)
    mine = lax.axis_index("blocks")
    partial_value = jnp.zeros((width, width * block_count), jnp.float32)
    current = centred
    for step in range(block_count):
        if step > 0:
            ring = [(i, (i + 1) % block_count) for i in range(block_count)]
            current = lax.ppermute(current, "blocks", ring)
        source = (mine - step) % block_count
        partial_value = lax.dynamic_update_slice_in_dim(
            partial_value, cross_gram(centred, current), source * width, 1
        )
    tile = lax.psum_scatter(partial_value, "cells", scatter_dimension=1, tiled=True)
    column_start = lax.axis_index("cells") * tile.shape[1]
    column_variance = lax.dynamic_slice_in_dim(every_variance, column_start, tile.shape[1])
    row_scale, column_scale = 1.0 / jnp.sqrt(variance), 1.0 / jnp.sqrt(column_variance)
    return power_six(tile * row_scale[:, None] * column_scale[None, :])


def solution(mesh):
    line = mesh.shape["cells"] == 4 and mesh.shape["blocks"] == 4
    return jax.shard_map(
        on_a_line if line else on_a_ring,
        mesh=mesh,
        in_specs=(P(("groups", "cells"), "blocks"),),
        out_specs=P(("groups", "blocks"), "cells"),
        check_vma=False,
    )
```

```python
import functools

import jax
import jax.numpy as jnp
from jax import lax
from jax.experimental import pallas as pl
from jax.experimental.pallas import tpu as pltpu
from jax.sharding import PartitionSpec as P

BOTH = ("cells", "blocks")
TILE = 256
FAR_WIDTHS = (2, 1, 1)
PAD = 16
f32, bf16 = jnp.float32, jnp.bfloat16
ANYWHERE = pl.BlockSpec(memory_space=pl.ANY)


def call(kernel, *, grid, in_specs, out_specs, out_shape, scratch=(), scalars=0, aliases=None, flops=1):
    return pl.pallas_call(
        kernel,
        grid_spec=pltpu.PrefetchScalarGridSpec(
            num_scalar_prefetch=scalars,
            grid=grid,
            in_specs=in_specs,
            out_specs=out_specs,
            scratch_shapes=scratch,
        ),
        out_shape=out_shape,
        input_output_aliases=aliases or {},
        cost_estimate=pl.CostEstimate(flops=flops, bytes_accessed=1, transcendentals=0),
        compiler_params=pltpu.CompilerParams(vmem_limit_bytes=48 << 20),
    )


def shape(*dims):
    return jax.ShapeDtypeStruct(dims, f32)


def split(value):
    high = value.astype(bf16)
    return high, (value - high.astype(f32)).astype(bf16)


def centre_kernel(x_ref, centred_ref, turned_ref, mean_ref, spread_ref):
    value = x_ref[...].astype(f32)
    mean = jnp.sum(value, axis=0, keepdims=True) / value.shape[0]
    value = value - mean
    centred_ref[...] = value
    turned_ref[...] = value.T
    mean_ref[...] = mean
    spread_ref[...] = jnp.sum(value * value, axis=0, keepdims=True)


def centre(expression):
    rows, width = expression.shape
    column = pl.BlockSpec((rows, TILE), lambda g: (0, g))
    line = pl.BlockSpec((1, TILE), lambda g: (0, g))
    return call(
        centre_kernel,
        grid=(width // TILE,),
        in_specs=[column],
        out_specs=[column, pl.BlockSpec((TILE, rows), lambda g: (g, 0)), line, line],
        out_shape=[shape(rows, width), shape(width, rows), shape(1, width), shape(1, width)],
    )(expression)


def copy_kernel(from_ref, to_ref):
    to_ref[...] = from_ref[...]


def columns(source, start, size, pad):
    rows = source.shape[0]
    tile = (rows + pad) // 2
    return call(
        copy_kernel,
        grid=(2,),
        in_specs=[pl.BlockSpec((tile, size), lambda i: (i, start // size))],
        out_specs=pl.BlockSpec((tile, size), lambda i: (i, 0)),
        out_shape=shape(rows + pad, size),
    )(source)


def pass_on(value, *earlier):
    return call(
        lambda *refs: None,
        grid=(1,),
        in_specs=[ANYWHERE] * (1 + len(earlier)),
        out_specs=ANYWHERE,
        out_shape=shape(*value.shape),
        aliases={0: 0},
    )(value, *earlier)


def gram_kernel(roles, cores, turned, adds, role_ref, *refs):
    lefts, rights = refs[: cores * roles], refs[cores * roles : cores * (roles + 1)]
    before_ref = refs[cores * (roles + 1)]
    out_ref, left_high, left_low, right_high, right_low = refs[-5:]
    cells = lefts[0].shape[1]

    @pl.when(pl.program_id(0) == 0)
    def _():
        for core, ref in enumerate(rights):
            span = slice(core * cells, (core + 1) * cells)
            at = (slice(None), span) if turned else span
            right_high[at], right_low[at] = split(ref[...])

    for role in range(roles):

        @pl.when(role_ref[0] == role if roles > 1 else True)
        def _():
            for core in range(cores):
                at = (slice(None), slice(core * cells, (core + 1) * cells))
                left_high[at], left_low[at] = split(lefts[cores * role + core][...])

    contract = (((1,), (1 if turned else 0,)), ((), ()))

    def dot(left, right):
        return lax.dot_general(left, right, contract, preferred_element_type=f32)

    width = out_ref.shape[1]
    for start in range(0, width, 512):
        span = slice(start, min(start + 512, width))
        at = span if turned else (slice(None), span)
        high, low = right_high[at], right_low[at]
        total = dot(left_high[...], high) + (
            dot(left_high[...], low) + dot(left_low[...], high)
        )
        out_ref[:, span] = before_ref[:, span] + total if adds else total


def gram(role, lefts, rights, turned, earlier, rows=None, pad=0, before=None):
    width, cells = lefts[0].shape
    cores, adds = len(rights), before is not None
    roles, rows = len(lefts) // cores, rows or width
    size = rights[0].shape[0 if turned else 1]

    def left_spec(of_role):
        def index(i, role_ref):
            at = i + role_ref[1]
            return (jnp.where(role_ref[0] == of_role, at, 0) if roles > 1 else at), 0

        return pl.BlockSpec((TILE, cells), index)

    right_block = (size, cells) if turned else (cells, size)
    right_shape = (size, cores * cells) if turned else (cores * cells, size)
    out = pl.BlockSpec((TILE, size), lambda i, role_ref: (i, 0))
    return call(
        functools.partial(gram_kernel, roles, cores, turned, adds),
        scalars=1,
        grid=(rows // TILE,),
        in_specs=[left_spec(n // cores) for n in range(len(lefts))]
        + [pl.BlockSpec(right_block, lambda i, role_ref: (0, 0))] * cores
        + [out] * adds
        + [ANYWHERE] * len(earlier),
        out_specs=out,
        out_shape=shape(rows + pad, size),
        scratch=[pltpu.VMEM((TILE, cores * cells), bf16)] * 2 + [pltpu.VMEM(right_shape, bf16)] * 2,
    )(role, *lefts, *rights, *([before] if adds else []), *earlier)


def together(work, *given):
    like = jax.eval_shape(work, *given)
    zeros = lambda *_: jax.tree.map(lambda leaf: jnp.zeros(leaf.shape, leaf.dtype), like)
    return lax.cond(lax.axis_index("cells") >= 0, work, zeros, *given)


def power_six(ratio):
    half = (1.0 + ratio) * 0.5
    square = half * half
    return square * square * square


def add_kernel(*refs):
    refs[-1][...] = refs[0][...] + refs[1][...]


def add(left, right, *earlier):
    block = pl.BlockSpec((TILE, left.shape[1]), lambda i: (i, 0))
    return call(
        add_kernel,
        grid=(left.shape[0] // TILE,),
        in_specs=[block] * 2 + [ANYWHERE] * len(earlier),
        out_specs=block,
        out_shape=shape(*left.shape),
    )(left, right, *earlier)


def adjacency(left, right, rs, cs, row_moments, column_moments):
    between_shards = sum(row_moments[:, n : n + 1] * column_moments[n : n + 1] for n in range(4))
    return power_six((left + right) * rs * cs + between_shards)


def scale_specs(size, column):
    return [
        pl.BlockSpec((TILE, 1), lambda i, flags: (i, 0)),
        pl.BlockSpec((1, size), lambda i, flags: (0, column)),
        pl.BlockSpec((TILE, 8), lambda i, flags: (i, 0)),
        pl.BlockSpec((8, size), lambda i, flags: (0, column)),
    ]


def base_kernel(pieces, flags, *refs):
    (rs, cs, rm, cm, out_ref), refs = refs[-5:], iter(refs)
    in_first = 2 * pl.program_id(0) < pl.num_programs(0)
    for start, halves in pieces:
        left, right = next(refs)[...], next(refs)[...]
        if halves:
            left = jnp.where(in_first, left, next(refs)[...])
            right = jnp.where(in_first, right, next(refs)[...])
        at = (slice(None), slice(start, start + left.shape[1]))
        out_ref[at] = adjacency(left, right, rs[...], cs[at], rm[...], cm[at])


def base(flags, pieces, scales):
    width = scales[0].shape[0]
    arrays = [array for _, *parts in pieces for array in parts]

    def spec(array):
        steps = array.shape[0] // TILE
        return pl.BlockSpec((TILE, array.shape[1]), lambda i, flags: (i % steps, 0))

    return call(
        functools.partial(base_kernel, [(start, len(parts) == 4) for start, *parts in pieces]),
        scalars=1,
        grid=(width // TILE,),
        in_specs=[spec(array) for array in arrays] + scale_specs(width, 0),
        out_specs=pl.BlockSpec((TILE, width), lambda i, flags: (i, 0)),
        out_shape=shape(width, width),
    )(flags, *arrays, *scales)


def finish_kernel(flags, *refs):
    (rs, cs, rm, cm, before, out_ref), tiles = refs[-6:], refs[:-6]

    @pl.when(flags[1] == 0)
    def _():
        out_ref[...] = before[...]

    for outer in range(2):

        @pl.when(flags[1] == 1 + outer)
        def _():
            for n in range(len(tiles) // 3):
                merged, first, second = tiles[3 * n : 3 * n + 3]
                size = first.shape[1]
                at = (slice(None), slice(n * size, (n + 1) * size))
                left = (second if outer else merged)[...]
                out_ref[at] = adjacency(left, first[...], rs[...], cs[at], rm[...], cm[at])


def finish(flags, tiles, scales, before, start):
    width, size = before.shape[0], sum(tile[0].shape[1] for tile in tiles)
    here = pl.BlockSpec((TILE, size), lambda i, flags: (i, start // size))

    def spec(size, *kinds, column=0):
        def index(i, flags):
            used = functools.reduce(jnp.logical_or, [flags[1] == kind for kind in kinds])
            return jnp.where(used, i, 0), column

        return pl.BlockSpec((TILE, size), index)

    operands = [flags, *(array for tile in tiles for array in tile), *scales, before]
    in_specs = []
    for tile in tiles:
        in_specs += [spec(tile[0].shape[1], *kinds) for kinds in ((1,), (1, 2), (2,))]
    return call(
        finish_kernel,
        scalars=1,
        grid=(width // TILE,),
        in_specs=in_specs + scale_specs(size, start // size) + [spec(size, 0, column=start // size)],
        out_specs=here,
        out_shape=shape(width, width),
        aliases={len(operands) - 1: 0},
    )(*operands)


def cross_gram(left, right):
    return lax.dot_general(
        left,
        right,
        (((0,), (0,)), ((), ())),
        preferred_element_type=f32,
        precision=lax.Precision.HIGH,
    )


def pieces(width, shares):
    unit = width // sum(shares)
    starts = [unit * sum(shares[:i]) for i in range(len(shares))]
    return [(start, unit * share) for start, share in zip(starts, shares)]


def local_statistics(values):
    mean = jnp.sum(values, axis=0) / values.shape[0]
    shifted = values - mean[None, :]
    return shifted, mean, jnp.sum(shifted * shifted, axis=0)


def statistics(rows, mean, spread):
    shards = lax.all_gather(jnp.stack([mean, spread]), "cells")
    away = shards[:, 0] - jnp.mean(shards[:, 0], axis=0)[None, :]
    variance = jnp.sum(shards[:, 1], axis=0) + rows * jnp.sum(away * away, axis=0)
    return away, variance


def on_a_line(expression):
    rows, width = expression.shape
    z = lax.axis_index("blocks")
    k = lax.axis_index("cells")
    mid_of, far_of = (2, 2, 1, 1), (3, 3, 0, 0)
    own_owner, pair_owner = (0, 1, 2, 3), (1, 0, 3, 2)
    far_id = jnp.where(z < 2, 3, 0)
    outer = ((z == 0) | (z == 3)).astype(jnp.int32)
    kind = jnp.where(k == far_id, 5, 3) + outer
    kind = jnp.where(k == z, 0, jnp.where(k == (z ^ 1), 1 + k % 2, kind))
    flags = jnp.stack([kind, jnp.where(k == far_id, 1 + outer, 0)]).astype(jnp.int32)
    far_role = jnp.stack([(k % 2 != far_id % 2).astype(jnp.int32), 0])
    mid_role = jnp.stack([1 - far_role[0], 0])
    pair_half = jnp.stack([0, (k % 2) * (width // 2 // TILE)]).astype(jnp.int32)

    def between(part, pairs, name):
        with jax.named_scope(name):
            return lax.ppermute(part, BOTH, [(a * 4 + b, c * 4 + d) for (a, b), (c, d) in pairs])

    def along(part, pairs, name):
        with jax.named_scope(name):
            return lax.ppermute(part, "blocks", pairs)

    def other(part, name):
        return between(part, [((i, b), (i ^ 1, b)) for i in range(4) for b in range(4)], name)

    def to_lane(part, owner, name, cores=(0,)):
        pairs = [((owner[b] ^ 2 ^ c, b), (owner[b] ^ c, b)) for b in range(4) for c in cores]
        return between(part, pairs, name)

    def onward(part, owner, name):
        pairs = [((owner[b] ^ 2, b), (owner[b], b)) for b in (1, 2)]
        pairs += [((owner[b] ^ 3, b), (owner[b], b ^ 1)) for b in (1, 2)]
        pairs += [((owner[b] ^ 1, b), (owner[b] ^ 1, b ^ 1)) for b in (1, 2)]
        return between(part, pairs, name)

    def folded(part, owner, name):
        return between(part, [((owner[b] ^ 1, b), (owner[b], b)) for b in (0, 3)], name)

    centred, turned, mean, spread = centre(expression)
    mid_got = along(centred, [(1, 2), (2, 1)], "mid_block")
    pair_got = along(turned, [(0, 1), (1, 0), (2, 3), (3, 2)], "pair_block")
    far = pieces(width, FAR_WIDTHS)
    far_parts = [columns(centred, *piece, pad) for piece, pad in zip(far, (PAD, PAD, 4 * PAD))]
    away, variance = statistics(rows, mean[0], spread[0])
    mine = jnp.concatenate([away, variance[None, :], jnp.zeros((11, width), f32)])

    def own_work(turned, earlier):
        own = turned, other(turned, "own_other")
        return gram(mid_role, own, own, True, earlier), own[1]

    def in_turn(role, own, pair, got, got_other, earlier, pad=0):
        mine = gram(role, (own[0], pair[0]), (got,), False, earlier)
        return gram(role, (own[1], pair[1]), (got_other,), False, (), pad=pad, before=mine)

    def mid_work(own, pair_got, mid_got, earlier):
        pair = pair_got, other(pair_got, "pair_other")
        mid_other = other(mid_got, "mid_other")
        return in_turn(mid_role, own, pair, mid_got, mid_other, earlier), pair[1]

    def first_far_work(own, pair, got, pair_sum, earlier):
        right = got, other(got, "far_other")
        total = gram(far_role, own + pair, right, False, earlier, pad=PAD)
        return total, other(pass_on(pair_sum, right[1]), "pair_fold")

    def far_work(own, pair, got, earlier):
        right = got, other(got, "far_other")
        return gram(far_role, own + pair, right, False, earlier, pad=PAD)

    own_sum, own_other = together(own_work, turned, (mine, *far_parts))
    own = turned, own_other
    pairs = [((a, b), (b, a)) for a in range(4) for b in range(4) if a != b]
    column = between(mine, pairs, "moments")
    far_got = []
    for part in far_parts:
        part = pass_on(part, pair_got, mid_got, column)
        far_got.append(along(part, [(0, 2), (3, 1)], "far_block"))
    own_far = to_lane(own_sum, own_owner, "own_lane")
    mid_sum, pair_other = together(mid_work, own, pair_got, mid_got, (own_sum,))
    pair = pair_got, pair_other
    mid_far = onward(mid_sum, mid_of, "mid_sum")
    pair_sum = gram(pair_half, own, pair, True, (mid_sum, own_far), rows=width // 2, pad=PAD)
    pair_far = to_lane(pair_sum, pair_owner, "pair_lane", cores=(0, 1))
    first_sum, pair_fold = together(
        first_far_work, own, pair, far_got[0], pair_sum, (pair_sum,)
    )
    first_far = onward(first_sum, far_of, "far_sum")
    second_sum = together(far_work, own, pair, far_got[1], (first_sum,))
    second_far = onward(second_sum, far_of, "far_sum")
    last_sum = together(far_work, own, pair, far_got[2], (second_sum,))
    last_far = onward(last_sum, far_of, "far_sum")

    column = jnp.where(k == z, mine, column)
    row_scale = 1.0 / jnp.sqrt(variance)
    column_scale = 1.0 / jnp.sqrt(column[4])
    row_moments = rows * jnp.pad(away * row_scale[None, :], ((0, 4), (0, 0))).T
    column_moments = jnp.pad(column[:4] * column_scale[None, :], ((0, 4), (0, 0)))
    scales = row_scale[:, None], column_scale[None, :], row_moments, column_moments

    def base_work(near, mid, far, scales):
        own_sum, own_far, pair_sum, pair_far, pair_fold = near
        pair_far_fold = other(pair_far, "pair_fold")
        cases = [
            [(0, own_sum, own_far)],
            [(0, pair_sum, pair_far, pair_fold, pair_far_fold)],
            [(0, pair_fold, pair_far_fold, pair_sum, pair_far)],
            [(0, *mid)],
            [(0, folded(mid[1], mid_of, "mid_fold"), mid[1])],
            [(0, *far)],
            [(0, folded(far[1], far_of, "far_fold"), far[1])],
        ]
        return lax.switch(flags[0], [lambda case=case: base(flags, case, scales) for case in cases])

    def last_work(fars, scales, result):
        tiles = [(*tile, folded(tile[1], far_of, "far_fold")) for tile in fars]
        return finish(flags, tiles, scales, result, far[1][0])

    near = own_sum, own_far, pair_sum, pair_far, pair_fold
    result = together(base_work, near, (mid_sum, mid_far), (first_sum, first_far), scales)
    fars = (second_sum, second_far), (last_sum, last_far)
    return together(last_work, fars, scales, result)


def on_a_ring(expression):
    rows, width = expression.shape
    block_count = lax.axis_size("blocks")
    shifted, mean, spread = local_statistics(expression.astype(jnp.float32))
    away, variance = statistics(rows, mean, spread)
    centred = shifted + lax.dynamic_index_in_dim(away, lax.axis_index("cells"), 0)
    every_variance = lax.all_gather(variance, "blocks", axis=0, tiled=True)
    mine = lax.axis_index("blocks")
    partial_value = jnp.zeros((width, width * block_count), jnp.float32)
    current = centred
    for step in range(block_count):
        if step > 0:
            ring = [(i, (i + 1) % block_count) for i in range(block_count)]
            current = lax.ppermute(current, "blocks", ring)
        source = (mine - step) % block_count
        partial_value = lax.dynamic_update_slice_in_dim(
            partial_value, cross_gram(centred, current), source * width, 1
        )
    tile = lax.psum_scatter(partial_value, "cells", scatter_dimension=1, tiled=True)
    column_start = lax.axis_index("cells") * tile.shape[1]
    column_variance = lax.dynamic_slice_in_dim(every_variance, column_start, tile.shape[1])
    row_scale, column_scale = 1.0 / jnp.sqrt(variance), 1.0 / jnp.sqrt(column_variance)
    return power_six(tile * row_scale[:, None] * column_scale[None, :])


def solution(mesh):
    line = mesh.shape["cells"] == 4 and mesh.shape["blocks"] == 4
    return jax.shard_map(
        on_a_line if line else on_a_ring,
        mesh=mesh,
        in_specs=(P(("groups", "cells"), "blocks"),),
        out_specs=P(("groups", "blocks"), "cells"),
        check_vma=False,
    )
```

```python
import functools

import jax
import jax.numpy as jnp
from jax import lax
from jax.experimental import pallas as pl
from jax.experimental.pallas import tpu as pltpu
from jax.sharding import PartitionSpec as P

BOTH = ("cells", "blocks")
TILE = 256
WIDE = 512
FAR_WIDTHS = (2, 1, 1)
PAD = 16
f32, bf16 = jnp.float32, jnp.bfloat16
ANYWHERE = pl.BlockSpec(memory_space=pl.ANY)


def call(kernel, *, grid, in_specs, out_specs, out_shape, scratch=(), scalars=0, aliases=None, vmem=40, flops=1):
    return pl.pallas_call(
        kernel,
        grid_spec=pltpu.PrefetchScalarGridSpec(
            num_scalar_prefetch=scalars,
            grid=grid,
            in_specs=in_specs,
            out_specs=out_specs,
            scratch_shapes=scratch,
        ),
        out_shape=out_shape,
        input_output_aliases=aliases or {},
        cost_estimate=pl.CostEstimate(flops=flops, bytes_accessed=1, transcendentals=0),
        compiler_params=pltpu.CompilerParams(vmem_limit_bytes=vmem << 20),
    )


def shape(*dims):
    return jax.ShapeDtypeStruct(dims, f32)


def split(value):
    high = value.astype(bf16)
    return high, (value - high.astype(f32)).astype(bf16)


def centre_kernel(x_ref, centred_ref, turned_ref, mean_ref, spread_ref):
    value = x_ref[...].astype(f32)
    mean = jnp.sum(value, axis=0, keepdims=True) / value.shape[0]
    value = value - mean
    centred_ref[...] = value
    turned_ref[...] = value.T
    mean_ref[...] = mean
    spread_ref[...] = jnp.sum(value * value, axis=0, keepdims=True)


def centre(expression):
    rows, width = expression.shape
    column = pl.BlockSpec((rows, TILE), lambda g: (0, g))
    line = pl.BlockSpec((1, TILE), lambda g: (0, g))
    return call(
        centre_kernel,
        grid=(width // TILE,),
        in_specs=[column],
        out_specs=[column, pl.BlockSpec((TILE, rows), lambda g: (g, 0)), line, line],
        out_shape=[shape(rows, width), shape(width, rows), shape(1, width), shape(1, width)],
        vmem=60,
    )(expression)


def copy_kernel(from_ref, to_ref):
    to_ref[...] = from_ref[...]


def columns(source, start, size, pad):
    rows = source.shape[0]
    tile = (rows + pad) // 2
    return call(
        copy_kernel,
        grid=(2,),
        in_specs=[pl.BlockSpec((tile, size), lambda i: (i, start // size))],
        out_specs=pl.BlockSpec((tile, size), lambda i: (i, 0)),
        out_shape=shape(rows + pad, size),
    )(source)


def pass_on(value, *earlier):
    return call(
        lambda *refs: None,
        grid=(1,),
        in_specs=[ANYWHERE] * (1 + len(earlier)),
        out_specs=ANYWHERE,
        out_shape=shape(*value.shape),
        aliases={0: 0},
    )(value, *earlier)


def gram_kernel(roles, cores, turned, adds, role_ref, *refs):
    lefts, rights = refs[: cores * roles], refs[cores * roles : cores * (roles + 1)]
    before_ref = refs[cores * (roles + 1)]
    out_ref, left_high, left_low, right_high, right_low = refs[-5:]
    cells = lefts[0].shape[1]

    @pl.when(pl.program_id(0) == 0)
    def _():
        for core, ref in enumerate(rights):
            span = slice(core * cells, (core + 1) * cells)
            at = (slice(None), span) if turned else span
            right_high[at], right_low[at] = split(ref[...])

    for role in range(roles):

        @pl.when(role_ref[0] == role if roles > 1 else True)
        def _():
            for core in range(cores):
                at = (slice(None), slice(core * cells, (core + 1) * cells))
                left_high[at], left_low[at] = split(lefts[cores * role + core][...])

    contract = (((1,), (1 if turned else 0,)), ((), ()))

    def dot(left, right):
        return lax.dot_general(left, right, contract, preferred_element_type=f32)

    width = out_ref.shape[1]
    for start in range(0, width, 512):
        span = slice(start, min(start + 512, width))
        at = span if turned else (slice(None), span)
        high, low = right_high[at], right_low[at]
        total = dot(left_high[...], high) + (
            dot(left_high[...], low) + dot(left_low[...], high)
        )
        out_ref[:, span] = before_ref[:, span] + total if adds else total


def gram(role, lefts, rights, turned, earlier, rows=None, pad=0, before=None):
    width, cells = lefts[0].shape
    cores, adds = len(rights), before is not None
    roles, rows = len(lefts) // cores, rows or width
    size = rights[0].shape[0 if turned else 1]

    def left_spec(of_role):
        def index(i, role_ref):
            at = i + role_ref[1]
            return (jnp.where(role_ref[0] == of_role, at, 0) if roles > 1 else at), 0

        return pl.BlockSpec((TILE, cells), index)

    right_block = (size, cells) if turned else (cells, size)
    right_shape = (size, cores * cells) if turned else (cores * cells, size)
    out = pl.BlockSpec((TILE, size), lambda i, role_ref: (i, 0))
    return call(
        functools.partial(gram_kernel, roles, cores, turned, adds),
        scalars=1,
        grid=(rows // TILE,),
        in_specs=[left_spec(n // cores) for n in range(len(lefts))]
        + [pl.BlockSpec(right_block, lambda i, role_ref: (0, 0))] * cores
        + [out] * adds
        + [ANYWHERE] * len(earlier),
        out_specs=out,
        out_shape=shape(rows + pad, size),
        scratch=[pltpu.VMEM((TILE, cores * cells), bf16)] * 2 + [pltpu.VMEM(right_shape, bf16)] * 2,
    )(role, *lefts, *rights, *([before] if adds else []), *earlier)


def together(work, *given):
    like = jax.eval_shape(work, *given)
    zeros = lambda *_: jax.tree.map(lambda leaf: jnp.zeros(leaf.shape, leaf.dtype), like)
    return lax.cond(lax.axis_index("cells") >= 0, work, zeros, *given)


def power_six(ratio):
    half = (1.0 + ratio) * 0.5
    square = half * half
    return square * square * square


def add_kernel(*refs):
    refs[-1][...] = refs[0][...] + refs[1][...]


def add(left, right, *earlier):
    block = pl.BlockSpec((TILE, left.shape[1]), lambda i: (i, 0))
    return call(
        add_kernel,
        grid=(left.shape[0] // TILE,),
        in_specs=[block] * 2 + [ANYWHERE] * len(earlier),
        out_specs=block,
        out_shape=shape(*left.shape),
    )(left, right, *earlier)


def adjacency(left, right, rs, cs, row_moments, column_moments):
    between_shards = sum(row_moments[:, n : n + 1] * column_moments[n : n + 1] for n in range(4))
    return power_six((left + right) * rs * cs + between_shards)


def scale_specs(size, column):
    return [
        pl.BlockSpec((WIDE, 1), lambda i, flags: (i, 0)),
        pl.BlockSpec((1, size), lambda i, flags: (0, column)),
        pl.BlockSpec((WIDE, 8), lambda i, flags: (i, 0)),
        pl.BlockSpec((8, size), lambda i, flags: (0, column)),
    ]


def base_kernel(pieces, flags, *refs):
    (rs, cs, rm, cm, out_ref), refs = refs[-5:], iter(refs)
    in_first = 2 * pl.program_id(0) < pl.num_programs(0)
    for start, halves in pieces:
        left, right = next(refs)[...], next(refs)[...]
        if halves:
            left = jnp.where(in_first, left, next(refs)[...])
            right = jnp.where(in_first, right, next(refs)[...])
        at = (slice(None), slice(start, start + left.shape[1]))
        out_ref[at] = adjacency(left, right, rs[...], cs[at], rm[...], cm[at])


def base(flags, pieces, scales):
    width = scales[0].shape[0]
    arrays = [array for _, *parts in pieces for array in parts]

    def spec(array):
        steps = array.shape[0] // WIDE
        return pl.BlockSpec((WIDE, array.shape[1]), lambda i, flags: (i % steps, 0))

    return call(
        functools.partial(base_kernel, [(start, len(parts) == 4) for start, *parts in pieces]),
        scalars=1,
        grid=(width // WIDE,),
        in_specs=[spec(array) for array in arrays] + scale_specs(width, 0),
        out_specs=pl.BlockSpec((WIDE, width), lambda i, flags: (i, 0)),
        out_shape=shape(width, width),
    )(flags, *arrays, *scales)


def finish_kernel(flags, *refs):
    (rs, cs, rm, cm, before, out_ref), tiles = refs[-6:], refs[:-6]

    @pl.when(flags[1] == 0)
    def _():
        out_ref[...] = before[...]

    for outer in range(2):

        @pl.when(flags[1] == 1 + outer)
        def _():
            for n in range(len(tiles) // 3):
                merged, first, second = tiles[3 * n : 3 * n + 3]
                size = first.shape[1]
                at = (slice(None), slice(n * size, (n + 1) * size))
                left = (second if outer else merged)[...]
                out_ref[at] = adjacency(left, first[...], rs[...], cs[at], rm[...], cm[at])


def finish(flags, tiles, scales, before, start):
    width, size = before.shape[0], sum(tile[0].shape[1] for tile in tiles)
    here = pl.BlockSpec((WIDE, size), lambda i, flags: (i, start // size))

    def spec(size, *kinds, column=0):
        def index(i, flags):
            used = functools.reduce(jnp.logical_or, [flags[1] == kind for kind in kinds])
            return jnp.where(used, i, 0), column

        return pl.BlockSpec((WIDE, size), index)

    operands = [flags, *(array for tile in tiles for array in tile), *scales, before]
    in_specs = []
    for tile in tiles:
        in_specs += [spec(tile[0].shape[1], *kinds) for kinds in ((1,), (1, 2), (2,))]
    return call(
        finish_kernel,
        scalars=1,
        grid=(width // WIDE,),
        in_specs=in_specs + scale_specs(size, start // size) + [spec(size, 0, column=start // size)],
        out_specs=here,
        out_shape=shape(width, width),
        aliases={len(operands) - 1: 0},
    )(*operands)


def cross_gram(left, right):
    return lax.dot_general(
        left,
        right,
        (((0,), (0,)), ((), ())),
        preferred_element_type=f32,
        precision=lax.Precision.HIGH,
    )


def pieces(width, shares):
    unit = width // sum(shares)
    starts = [unit * sum(shares[:i]) for i in range(len(shares))]
    return [(start, unit * share) for start, share in zip(starts, shares)]


def local_statistics(values):
    mean = jnp.sum(values, axis=0) / values.shape[0]
    shifted = values - mean[None, :]
    return shifted, mean, jnp.sum(shifted * shifted, axis=0)


def statistics(rows, mean, spread):
    shards = lax.all_gather(jnp.stack([mean, spread]), "cells")
    away = shards[:, 0] - jnp.mean(shards[:, 0], axis=0)[None, :]
    variance = jnp.sum(shards[:, 1], axis=0) + rows * jnp.sum(away * away, axis=0)
    return away, variance


def on_a_line(expression):
    rows, width = expression.shape
    z = lax.axis_index("blocks")
    k = lax.axis_index("cells")
    mid_of, far_of = (2, 2, 1, 1), (3, 3, 0, 0)
    own_owner, pair_owner = (0, 1, 2, 3), (1, 0, 3, 2)
    far_id = jnp.where(z < 2, 3, 0)
    outer = ((z == 0) | (z == 3)).astype(jnp.int32)
    kind = jnp.where(k == far_id, 5, 3) + outer
    kind = jnp.where(k == z, 0, jnp.where(k == (z ^ 1), 1 + k % 2, kind))
    flags = jnp.stack([kind, jnp.where(k == far_id, 1 + outer, 0)]).astype(jnp.int32)
    far_role = jnp.stack([(k % 2 != far_id % 2).astype(jnp.int32), 0])
    mid_role = jnp.stack([1 - far_role[0], 0])
    pair_half = jnp.stack([0, (k % 2) * (width // 2 // TILE)]).astype(jnp.int32)

    def between(part, pairs, name):
        with jax.named_scope(name):
            return lax.ppermute(part, BOTH, [(a * 4 + b, c * 4 + d) for (a, b), (c, d) in pairs])

    def along(part, pairs, name):
        with jax.named_scope(name):
            return lax.ppermute(part, "blocks", pairs)

    def other(part, name):
        return between(part, [((i, b), (i ^ 1, b)) for i in range(4) for b in range(4)], name)

    def to_lane(part, owner, name, cores=(0,)):
        pairs = [((owner[b] ^ 2 ^ c, b), (owner[b] ^ c, b)) for b in range(4) for c in cores]
        return between(part, pairs, name)

    def onward(part, owner, name):
        pairs = [((owner[b] ^ 2, b), (owner[b], b)) for b in (1, 2)]
        pairs += [((owner[b] ^ 3, b), (owner[b], b ^ 1)) for b in (1, 2)]
        pairs += [((owner[b] ^ 1, b), (owner[b] ^ 1, b ^ 1)) for b in (1, 2)]
        return between(part, pairs, name)

    def folded(part, owner, name):
        return between(part, [((owner[b] ^ 1, b), (owner[b], b)) for b in (0, 3)], name)

    centred, turned, mean, spread = centre(expression)
    mid_got = along(centred, [(1, 2), (2, 1)], "mid_block")
    pair_got = along(turned, [(0, 1), (1, 0), (2, 3), (3, 2)], "pair_block")
    far = pieces(width, FAR_WIDTHS)
    far_parts = [columns(centred, *piece, pad) for piece, pad in zip(far, (PAD, PAD, 4 * PAD))]
    away, variance = statistics(rows, mean[0], spread[0])
    mine = jnp.concatenate([away, variance[None, :], jnp.zeros((11, width), f32)])

    def own_work(turned, earlier):
        own = turned, other(turned, "own_other")
        return gram(mid_role, own, own, True, earlier), own[1]

    def in_turn(role, own, pair, got, got_other, earlier, pad=0):
        mine = gram(role, (own[0], pair[0]), (got,), False, earlier)
        return gram(role, (own[1], pair[1]), (got_other,), False, (), pad=pad, before=mine)

    def mid_work(own, pair_got, mid_got, earlier):
        pair = pair_got, other(pair_got, "pair_other")
        mid_other = other(mid_got, "mid_other")
        return in_turn(mid_role, own, pair, mid_got, mid_other, earlier), pair[1]

    def first_far_work(own, pair, got, pair_sum, earlier):
        right = got, other(got, "far_other")
        total = gram(far_role, own + pair, right, False, earlier, pad=PAD)
        return total, other(pass_on(pair_sum, right[1]), "pair_fold")

    def far_work(own, pair, got, earlier):
        right = got, other(got, "far_other")
        return gram(far_role, own + pair, right, False, earlier, pad=PAD)

    own_sum, own_other = together(own_work, turned, (mine, *far_parts))
    own = turned, own_other
    pairs = [((a, b), (b, a)) for a in range(4) for b in range(4) if a != b]
    column = between(mine, pairs, "moments")
    far_got = []
    for part in far_parts:
        part = pass_on(part, pair_got, mid_got, column)
        far_got.append(along(part, [(0, 2), (3, 1)], "far_block"))
    own_far = to_lane(own_sum, own_owner, "own_lane")
    mid_sum, pair_other = together(mid_work, own, pair_got, mid_got, (own_sum,))
    pair = pair_got, pair_other
    mid_far = onward(mid_sum, mid_of, "mid_sum")
    pair_sum = gram(pair_half, own, pair, True, (mid_sum, own_far), rows=width // 2, pad=PAD)
    pair_far = to_lane(pair_sum, pair_owner, "pair_lane", cores=(0, 1))
    first_sum, pair_fold = together(
        first_far_work, own, pair, far_got[0], pair_sum, (pair_sum,)
    )
    first_far = onward(first_sum, far_of, "far_sum")
    second_sum = together(far_work, own, pair, far_got[1], (first_sum,))
    second_far = onward(second_sum, far_of, "far_sum")
    last_sum = together(far_work, own, pair, far_got[2], (second_sum,))
    last_far = onward(last_sum, far_of, "far_sum")

    column = jnp.where(k == z, mine, column)
    row_scale = 1.0 / jnp.sqrt(variance)
    column_scale = 1.0 / jnp.sqrt(column[4])
    row_moments = rows * jnp.pad(away * row_scale[None, :], ((0, 4), (0, 0))).T
    column_moments = jnp.pad(column[:4] * column_scale[None, :], ((0, 4), (0, 0)))
    scales = row_scale[:, None], column_scale[None, :], row_moments, column_moments

    def base_work(near, mid, far, scales):
        own_sum, own_far, pair_sum, pair_far, pair_fold = near
        pair_far_fold = other(pair_far, "pair_fold")
        cases = [
            [(0, own_sum, own_far)],
            [(0, pair_sum, pair_far, pair_fold, pair_far_fold)],
            [(0, pair_fold, pair_far_fold, pair_sum, pair_far)],
            [(0, *mid)],
            [(0, folded(mid[1], mid_of, "mid_fold"), mid[1])],
            [(0, *far)],
            [(0, folded(far[1], far_of, "far_fold"), far[1])],
        ]
        return lax.switch(flags[0], [lambda case=case: base(flags, case, scales) for case in cases])

    def last_work(fars, scales, result):
        tiles = [(*tile, folded(tile[1], far_of, "far_fold")) for tile in fars]
        return finish(flags, tiles, scales, result, far[1][0])

    near = own_sum, own_far, pair_sum, pair_far, pair_fold
    result = together(base_work, near, (mid_sum, mid_far), (first_sum, first_far), scales)
    fars = (second_sum, second_far), (last_sum, last_far)
    return together(last_work, fars, scales, result)


def on_a_ring(expression):
    rows, width = expression.shape
    block_count = lax.axis_size("blocks")
    shifted, mean, spread = local_statistics(expression.astype(jnp.float32))
    away, variance = statistics(rows, mean, spread)
    centred = shifted + lax.dynamic_index_in_dim(away, lax.axis_index("cells"), 0)
    every_variance = lax.all_gather(variance, "blocks", axis=0, tiled=True)
    mine = lax.axis_index("blocks")
    partial_value = jnp.zeros((width, width * block_count), jnp.float32)
    current = centred
    for step in range(block_count):
        if step > 0:
            ring = [(i, (i + 1) % block_count) for i in range(block_count)]
            current = lax.ppermute(current, "blocks", ring)
        source = (mine - step) % block_count
        partial_value = lax.dynamic_update_slice_in_dim(
            partial_value, cross_gram(centred, current), source * width, 1
        )
    tile = lax.psum_scatter(partial_value, "cells", scatter_dimension=1, tiled=True)
    column_start = lax.axis_index("cells") * tile.shape[1]
    column_variance = lax.dynamic_slice_in_dim(every_variance, column_start, tile.shape[1])
    row_scale, column_scale = 1.0 / jnp.sqrt(variance), 1.0 / jnp.sqrt(column_variance)
    return power_six(tile * row_scale[:, None] * column_scale[None, :])


def solution(mesh):
    line = mesh.shape["cells"] == 4 and mesh.shape["blocks"] == 4
    return jax.shard_map(
        on_a_line if line else on_a_ring,
        mesh=mesh,
        in_specs=(P(("groups", "cells"), "blocks"),),
        out_specs=P(("groups", "blocks"), "cells"),
        check_vma=False,
    )
```

```python
import functools

import jax
import jax.numpy as jnp
from jax import lax
from jax.experimental import pallas as pl
from jax.experimental.pallas import tpu as pltpu
from jax.sharding import PartitionSpec as P

BOTH = ("cells", "blocks")
TILE = 256
WIDE = 512
FAR_WIDTHS = (2, 1, 1)
PAD = 16
f32, bf16 = jnp.float32, jnp.bfloat16
ANYWHERE = pl.BlockSpec(memory_space=pl.ANY)


def call(kernel, *, grid, in_specs, out_specs, out_shape, scratch=(), scalars=0, aliases=None, vmem=40, flops=1):
    return pl.pallas_call(
        kernel,
        grid_spec=pltpu.PrefetchScalarGridSpec(
            num_scalar_prefetch=scalars,
            grid=grid,
            in_specs=in_specs,
            out_specs=out_specs,
            scratch_shapes=scratch,
        ),
        out_shape=out_shape,
        input_output_aliases=aliases or {},
        cost_estimate=pl.CostEstimate(flops=flops, bytes_accessed=1, transcendentals=0),
        compiler_params=pltpu.CompilerParams(vmem_limit_bytes=vmem << 20),
    )


def shape(*dims):
    return jax.ShapeDtypeStruct(dims, f32)


def split(value):
    high = value.astype(bf16)
    return high, (value - high.astype(f32)).astype(bf16)


def centre_kernel(x_ref, centred_ref, turned_ref, mean_ref, spread_ref):
    value = x_ref[...].astype(f32)
    mean = jnp.sum(value, axis=0, keepdims=True) / value.shape[0]
    value = value - mean
    centred_ref[...] = value
    turned_ref[...] = value.T
    mean_ref[...] = mean
    spread_ref[...] = jnp.sum(value * value, axis=0, keepdims=True)


def centre(expression):
    rows, width = expression.shape
    column = pl.BlockSpec((rows, TILE), lambda g: (0, g))
    line = pl.BlockSpec((1, TILE), lambda g: (0, g))
    return call(
        centre_kernel,
        grid=(width // TILE,),
        in_specs=[column],
        out_specs=[column, pl.BlockSpec((TILE, rows), lambda g: (g, 0)), line, line],
        out_shape=[shape(rows, width), shape(width, rows), shape(1, width), shape(1, width)],
        vmem=60,
    )(expression)


def copy_kernel(from_ref, to_ref):
    to_ref[...] = from_ref[...]


def columns(source, start, size, pad):
    rows = source.shape[0]
    tile = (rows + pad) // 2
    return call(
        copy_kernel,
        grid=(2,),
        in_specs=[pl.BlockSpec((tile, size), lambda i: (i, start // size))],
        out_specs=pl.BlockSpec((tile, size), lambda i: (i, 0)),
        out_shape=shape(rows + pad, size),
    )(source)


def pass_on(value, *earlier):
    return call(
        lambda *refs: None,
        grid=(1,),
        in_specs=[ANYWHERE] * (1 + len(earlier)),
        out_specs=ANYWHERE,
        out_shape=shape(*value.shape),
        aliases={0: 0},
    )(value, *earlier)


def gram_kernel(roles, cores, turned, adds, role_ref, *refs):
    lefts, rights = refs[: cores * roles], refs[cores * roles : cores * (roles + 1)]
    before_ref = refs[cores * (roles + 1)]
    out_ref, left_high, left_low, right_high, right_low = refs[-5:]
    cells = lefts[0].shape[1]

    @pl.when(pl.program_id(0) == 0)
    def _():
        for core, ref in enumerate(rights):
            span = slice(core * cells, (core + 1) * cells)
            at = (slice(None), span) if turned else span
            right_high[at], right_low[at] = split(ref[...])

    for role in range(roles):

        @pl.when(role_ref[0] == role if roles > 1 else True)
        def _():
            for core in range(cores):
                at = (slice(None), slice(core * cells, (core + 1) * cells))
                left_high[at], left_low[at] = split(lefts[cores * role + core][...])

    contract = (((1,), (1 if turned else 0,)), ((), ()))

    def dot(left, right):
        return lax.dot_general(left, right, contract, preferred_element_type=f32)

    width = out_ref.shape[1]
    for start in range(0, width, 512):
        span = slice(start, min(start + 512, width))
        at = span if turned else (slice(None), span)
        high, low = right_high[at], right_low[at]
        total = dot(left_high[...], high) + (
            dot(left_high[...], low) + dot(left_low[...], high)
        )
        out_ref[:, span] = before_ref[:, span] + total if adds else total


def gram(role, lefts, rights, turned, earlier, rows=None, pad=0, before=None, vmem=40):
    width, cells = lefts[0].shape
    cores, adds = len(rights), before is not None
    roles, rows = len(lefts) // cores, rows or width
    size = rights[0].shape[0 if turned else 1]

    def left_spec(of_role):
        def index(i, role_ref):
            at = i + role_ref[1]
            return (jnp.where(role_ref[0] == of_role, at, 0) if roles > 1 else at), 0

        return pl.BlockSpec((TILE, cells), index)

    right_block = (size, cells) if turned else (cells, size)
    right_shape = (size, cores * cells) if turned else (cores * cells, size)
    out = pl.BlockSpec((TILE, size), lambda i, role_ref: (i, 0))
    return call(
        functools.partial(gram_kernel, roles, cores, turned, adds),
        scalars=1,
        grid=(rows // TILE,),
        in_specs=[left_spec(n // cores) for n in range(len(lefts))]
        + [pl.BlockSpec(right_block, lambda i, role_ref: (0, 0))] * cores
        + [out] * adds
        + [ANYWHERE] * len(earlier),
        out_specs=out,
        out_shape=shape(rows + pad, size),
        scratch=[pltpu.VMEM((TILE, cores * cells), bf16)] * 2 + [pltpu.VMEM(right_shape, bf16)] * 2,
        vmem=vmem,
    )(role, *lefts, *rights, *([before] if adds else []), *earlier)


def together(work, *given):
    like = jax.eval_shape(work, *given)
    zeros = lambda *_: jax.tree.map(lambda leaf: jnp.zeros(leaf.shape, leaf.dtype), like)
    return lax.cond(lax.axis_index("cells") >= 0, work, zeros, *given)


def power_six(ratio):
    half = (1.0 + ratio) * 0.5
    square = half * half
    return square * square * square


def add_kernel(*refs):
    refs[-1][...] = refs[0][...] + refs[1][...]


def add(left, right, *earlier):
    block = pl.BlockSpec((TILE, left.shape[1]), lambda i: (i, 0))
    return call(
        add_kernel,
        grid=(left.shape[0] // TILE,),
        in_specs=[block] * 2 + [ANYWHERE] * len(earlier),
        out_specs=block,
        out_shape=shape(*left.shape),
    )(left, right, *earlier)


def adjacency(left, right, rs, cs, row_moments, column_moments):
    between_shards = sum(row_moments[:, n : n + 1] * column_moments[n : n + 1] for n in range(4))
    return power_six((left + right) * rs * cs + between_shards)


def scale_specs(size, column):
    return [
        pl.BlockSpec((WIDE, 1), lambda i, flags: (i, 0)),
        pl.BlockSpec((1, size), lambda i, flags: (0, column)),
        pl.BlockSpec((WIDE, 8), lambda i, flags: (i, 0)),
        pl.BlockSpec((8, size), lambda i, flags: (0, column)),
    ]


def base_kernel(pieces, flags, *refs):
    (rs, cs, rm, cm, out_ref), refs = refs[-5:], iter(refs)
    in_first = 2 * pl.program_id(0) < pl.num_programs(0)
    for start, halves in pieces:
        left, right = next(refs)[...], next(refs)[...]
        if halves:
            left = jnp.where(in_first, left, next(refs)[...])
            right = jnp.where(in_first, right, next(refs)[...])
        at = (slice(None), slice(start, start + left.shape[1]))
        out_ref[at] = adjacency(left, right, rs[...], cs[at], rm[...], cm[at])


def base(flags, pieces, scales):
    width = scales[0].shape[0]
    arrays = [array for _, *parts in pieces for array in parts]

    def spec(array):
        steps = array.shape[0] // WIDE
        return pl.BlockSpec((WIDE, array.shape[1]), lambda i, flags: (i % steps, 0))

    return call(
        functools.partial(base_kernel, [(start, len(parts) == 4) for start, *parts in pieces]),
        scalars=1,
        grid=(width // WIDE,),
        in_specs=[spec(array) for array in arrays] + scale_specs(width, 0),
        out_specs=pl.BlockSpec((WIDE, width), lambda i, flags: (i, 0)),
        out_shape=shape(width, width),
    )(flags, *arrays, *scales)


def finish_kernel(flags, *refs):
    (rs, cs, rm, cm, before, out_ref), tiles = refs[-6:], refs[:-6]

    @pl.when(flags[1] == 0)
    def _():
        out_ref[...] = before[...]

    for outer in range(2):

        @pl.when(flags[1] == 1 + outer)
        def _():
            for n in range(len(tiles) // 3):
                merged, first, second = tiles[3 * n : 3 * n + 3]
                size = first.shape[1]
                at = (slice(None), slice(n * size, (n + 1) * size))
                left = (second if outer else merged)[...]
                out_ref[at] = adjacency(left, first[...], rs[...], cs[at], rm[...], cm[at])


def finish(flags, tiles, scales, before, start):
    width, size = before.shape[0], sum(tile[0].shape[1] for tile in tiles)
    here = pl.BlockSpec((WIDE, size), lambda i, flags: (i, start // size))

    def spec(size, *kinds, column=0):
        def index(i, flags):
            used = functools.reduce(jnp.logical_or, [flags[1] == kind for kind in kinds])
            return jnp.where(used, i, 0), column

        return pl.BlockSpec((WIDE, size), index)

    operands = [flags, *(array for tile in tiles for array in tile), *scales, before]
    in_specs = []
    for tile in tiles:
        in_specs += [spec(tile[0].shape[1], *kinds) for kinds in ((1,), (1, 2), (2,))]
    return call(
        finish_kernel,
        scalars=1,
        grid=(width // WIDE,),
        in_specs=in_specs + scale_specs(size, start // size) + [spec(size, 0, column=start // size)],
        out_specs=here,
        out_shape=shape(width, width),
        aliases={len(operands) - 1: 0},
    )(*operands)


def cross_gram(left, right):
    return lax.dot_general(
        left,
        right,
        (((0,), (0,)), ((), ())),
        preferred_element_type=f32,
        precision=lax.Precision.HIGH,
    )


def pieces(width, shares):
    unit = width // sum(shares)
    starts = [unit * sum(shares[:i]) for i in range(len(shares))]
    return [(start, unit * share) for start, share in zip(starts, shares)]


def local_statistics(values):
    mean = jnp.sum(values, axis=0) / values.shape[0]
    shifted = values - mean[None, :]
    return shifted, mean, jnp.sum(shifted * shifted, axis=0)


def statistics(rows, mean, spread):
    shards = lax.all_gather(jnp.stack([mean, spread]), "cells")
    away = shards[:, 0] - jnp.mean(shards[:, 0], axis=0)[None, :]
    variance = jnp.sum(shards[:, 1], axis=0) + rows * jnp.sum(away * away, axis=0)
    return away, variance


def on_a_line(expression):
    rows, width = expression.shape
    z = lax.axis_index("blocks")
    k = lax.axis_index("cells")
    mid_of, far_of = (2, 2, 1, 1), (3, 3, 0, 0)
    own_owner, pair_owner = (0, 1, 2, 3), (1, 0, 3, 2)
    far_id = jnp.where(z < 2, 3, 0)
    outer = ((z == 0) | (z == 3)).astype(jnp.int32)
    kind = jnp.where(k == far_id, 5, 3) + outer
    kind = jnp.where(k == z, 0, jnp.where(k == (z ^ 1), 1 + k % 2, kind))
    flags = jnp.stack([kind, jnp.where(k == far_id, 1 + outer, 0)]).astype(jnp.int32)
    far_role = jnp.stack([(k % 2 != far_id % 2).astype(jnp.int32), 0])
    mid_role = jnp.stack([1 - far_role[0], 0])
    pair_half = jnp.stack([0, (k % 2) * (width // 2 // TILE)]).astype(jnp.int32)

    def between(part, pairs, name):
        with jax.named_scope(name):
            return lax.ppermute(part, BOTH, [(a * 4 + b, c * 4 + d) for (a, b), (c, d) in pairs])

    def along(part, pairs, name):
        with jax.named_scope(name):
            return lax.ppermute(part, "blocks", pairs)

    def other(part, name):
        return between(part, [((i, b), (i ^ 1, b)) for i in range(4) for b in range(4)], name)

    def to_lane(part, owner, name, cores=(0,)):
        pairs = [((owner[b] ^ 2 ^ c, b), (owner[b] ^ c, b)) for b in range(4) for c in cores]
        return between(part, pairs, name)

    def onward(part, owner, name):
        pairs = [((owner[b] ^ 2, b), (owner[b], b)) for b in (1, 2)]
        pairs += [((owner[b] ^ 3, b), (owner[b], b ^ 1)) for b in (1, 2)]
        pairs += [((owner[b] ^ 1, b), (owner[b] ^ 1, b ^ 1)) for b in (1, 2)]
        return between(part, pairs, name)

    def folded(part, owner, name):
        return between(part, [((owner[b] ^ 1, b), (owner[b], b)) for b in (0, 3)], name)

    centred, turned, mean, spread = centre(expression)
    mid_got = along(centred, [(1, 2), (2, 1)], "mid_block")
    pair_got = along(turned, [(0, 1), (1, 0), (2, 3), (3, 2)], "pair_block")
    far = pieces(width, FAR_WIDTHS)
    far_parts = [columns(centred, *piece, pad) for piece, pad in zip(far, (PAD, PAD, 2 * PAD))]
    away, variance = statistics(rows, mean[0], spread[0])
    mine = jnp.concatenate([away, variance[None, :], jnp.zeros((11, width), f32)])

    def own_work(turned, earlier):
        own = turned, other(turned, "own_other")
        return gram(mid_role, own, own, True, earlier), own[1]

    def in_turn(role, own, pair, got, got_other, earlier, pad=0):
        mine = gram(role, (own[0], pair[0]), (got,), False, earlier, vmem=60)
        return gram(role, (own[1], pair[1]), (got_other,), False, (), pad=pad, before=mine)

    def mid_work(own, pair_got, mid_got, earlier):
        pair = pair_got, other(pair_got, "pair_other")
        mid_other = other(mid_got, "mid_other")
        return in_turn(mid_role, own, pair, mid_got, mid_other, earlier), pair[1]

    def first_far_work(own, pair, got, pair_sum, earlier):
        right = got, other(got, "far_other")
        total = gram(far_role, own + pair, right, False, earlier, pad=PAD)
        return total, other(pass_on(pair_sum, right[1]), "pair_fold")

    def far_work(own, pair, got, earlier):
        right = got, other(got, "far_other")
        return gram(far_role, own + pair, right, False, earlier, pad=PAD)

    own_sum, own_other = together(own_work, turned, (mine, *far_parts))
    own = turned, own_other
    pairs = [((a, b), (b, a)) for a in range(4) for b in range(4) if a != b]
    column = between(mine, pairs, "moments")
    far_got = []
    for part in far_parts:
        part = pass_on(part, pair_got, mid_got, column)
        far_got.append(along(part, [(0, 2), (3, 1)], "far_block"))
    own_far = to_lane(own_sum, own_owner, "own_lane")
    mid_sum, pair_other = together(mid_work, own, pair_got, mid_got, (own_sum,))
    pair = pair_got, pair_other
    mid_far = onward(mid_sum, mid_of, "mid_sum")
    pair_sum = gram(pair_half, own, pair, True, (mid_sum, own_far), rows=width // 2, pad=PAD)
    pair_far = to_lane(pair_sum, pair_owner, "pair_lane", cores=(0, 1))
    first_sum, pair_fold = together(
        first_far_work, own, pair, far_got[0], pair_sum, (pair_sum,)
    )
    first_far = onward(first_sum, far_of, "far_sum")
    second_sum = together(far_work, own, pair, far_got[1], (first_sum,))
    second_far = onward(second_sum, far_of, "far_sum")
    last_sum = together(far_work, own, pair, far_got[2], (second_sum,))
    last_far = onward(last_sum, far_of, "far_sum")

    column = jnp.where(k == z, mine, column)
    row_scale = 1.0 / jnp.sqrt(variance)
    column_scale = 1.0 / jnp.sqrt(column[4])
    row_moments = rows * jnp.pad(away * row_scale[None, :], ((0, 4), (0, 0))).T
    column_moments = jnp.pad(column[:4] * column_scale[None, :], ((0, 4), (0, 0)))
    scales = row_scale[:, None], column_scale[None, :], row_moments, column_moments

    def base_work(near, mid, far, scales):
        own_sum, own_far, pair_sum, pair_far, pair_fold = near
        pair_far_fold = other(pair_far, "pair_fold")
        cases = [
            [(0, own_sum, own_far)],
            [(0, pair_sum, pair_far, pair_fold, pair_far_fold)],
            [(0, pair_fold, pair_far_fold, pair_sum, pair_far)],
            [(0, *mid)],
            [(0, folded(mid[1], mid_of, "mid_fold"), mid[1])],
            [(0, *far)],
            [(0, folded(far[1], far_of, "far_fold"), far[1])],
        ]
        return lax.switch(flags[0], [lambda case=case: base(flags, case, scales) for case in cases])

    def last_work(fars, scales, result):
        tiles = [(*tile, folded(tile[1], far_of, "far_fold")) for tile in fars]
        return finish(flags, tiles, scales, result, far[1][0])

    near = own_sum, own_far, pair_sum, pair_far, pair_fold
    result = together(base_work, near, (mid_sum, mid_far), (first_sum, first_far), scales)
    fars = (second_sum, second_far), (last_sum, last_far)
    return together(last_work, fars, scales, result)


def on_a_ring(expression):
    rows, width = expression.shape
    block_count = lax.axis_size("blocks")
    shifted, mean, spread = local_statistics(expression.astype(jnp.float32))
    away, variance = statistics(rows, mean, spread)
    centred = shifted + lax.dynamic_index_in_dim(away, lax.axis_index("cells"), 0)
    every_variance = lax.all_gather(variance, "blocks", axis=0, tiled=True)
    mine = lax.axis_index("blocks")
    partial_value = jnp.zeros((width, width * block_count), jnp.float32)
    current = centred
    for step in range(block_count):
        if step > 0:
            ring = [(i, (i + 1) % block_count) for i in range(block_count)]
            current = lax.ppermute(current, "blocks", ring)
        source = (mine - step) % block_count
        partial_value = lax.dynamic_update_slice_in_dim(
            partial_value, cross_gram(centred, current), source * width, 1
        )
    tile = lax.psum_scatter(partial_value, "cells", scatter_dimension=1, tiled=True)
    column_start = lax.axis_index("cells") * tile.shape[1]
    column_variance = lax.dynamic_slice_in_dim(every_variance, column_start, tile.shape[1])
    row_scale, column_scale = 1.0 / jnp.sqrt(variance), 1.0 / jnp.sqrt(column_variance)
    return power_six(tile * row_scale[:, None] * column_scale[None, :])


def solution(mesh):
    line = mesh.shape["cells"] == 4 and mesh.shape["blocks"] == 4
    return jax.shard_map(
        on_a_line if line else on_a_ring,
        mesh=mesh,
        in_specs=(P(("groups", "cells"), "blocks"),),
        out_specs=P(("groups", "blocks"), "cells"),
        check_vma=False,
    )
```
